256 devices in a mesh: section: 2 (over x_hi), expert: 64 (over z, y, x_lo), dp: 2 (over core).
Axes of the slice: x: 4 (x_hi: 2, x_lo: 2; x = x_hi * 2 + x_lo), y: 4, z: 8, core: 2. Of those that a mesh axis runs over, the one named last changes fastest.
Arguments:
- layer_input: bfloat16 [2, 2, 8192, 2048], P('section', 'dp', 'expert'), may hold values from -6 to 6
- grad_output: bfloat16 [2, 2, 8192, 2048], P('section', 'dp', 'expert'), may hold values from -3 to 3
- selections: int32 [2, 2, 16, 512], P('section', 'dp'), may hold values from 0 to 8191, as said below
- gate_values: float32 [2, 2, 16, 512], P('section', 'dp'), may hold values from 0.1 to 1
- gate_weight: bfloat16 [2, 64, 2048, 256], P('section', 'expert', 'dp'), may hold values from -0.125 to 0.125
- up_weight: bfloat16 [2, 64, 2048, 256], P('section', 'expert', 'dp'), may hold values from -0.125 to 0.125
- down_weight: bfloat16 [2, 64, 256, 2048], P('section', 'expert', None, 'dp'), may hold values from -0.1875 to 0.1875
Outputs:
- incoming_grad: bfloat16 [2, 2, 8192, 2048], P('section', 'dp', 'expert')
- gate_grad: float32 [2, 2, 16, 512], P('section', 'dp')
- gate_weight_grad: float32 [2, 64, 2048, 256], P('section', 'expert', 'dp')
- up_weight_grad: float32 [2, 64, 2048, 256], P('section', 'expert', 'dp')
- down_weight_grad: float32 [2, 64, 256, 2048], P('section', 'expert', None, 'dp')
The draws below stay inside these ranges and needn't reach their ends.
Inputs may be any that keep to these rules, and one draw needn't show every extreme that they name: Row e of selections[s, b] lists 512 distinct tokens of micro-batch b, in no particular order. Of the 128 tokens k * 128 to (k + 1) * 128 - 1, one expert takes at most 16, and every expert takes exactly 16 from some such block.
All inputs are finite; a program needn't handle non-finite values.
Results may differ from the reference program's by a relative error of at most 0.0085.
Values may be sent and summed in bfloat16 or wider, within the bound.
A program may use at most 128 MiB of HBM per device.

```python
import math
import jax
import jax.numpy as jnp
from jax import lax

D = 2048
HID_DEV = 256
SPLIT = 4
HID = 1024
TOK_DEV = 128
TOKENS = 8192
EXPERTS = 16
CAP = 512
SECTIONS = 2
BATCHES = 2


def permute_block(block_key):
    return jax.random.permutation(block_key, TOK_DEV)


def choose_tokens(expert_key):
    blocks = TOKENS // TOK_DEV
    half_blocks = blocks // 2
    mean_take = TOK_DEV // 16
    key_order, key_spread, key_rank, key_shuffle = jax.random.split(expert_key, 4)
    block_order = jax.random.permutation(key_order, blocks)
    deviation = jax.random.randint(key_spread, (half_blocks,), 0, mean_take + 1)
    deviation = deviation.at[0].set(mean_take)
    block_counts = jnp.zeros((blocks,), jnp.int32)
    block_counts = block_counts.at[block_order[:half_blocks]].set(mean_take + deviation)
    block_counts = block_counts.at[block_order[half_blocks:]].set(mean_take - deviation)
    ranking = jax.vmap(permute_block)(jax.random.split(key_rank, blocks))
    positions = jnp.broadcast_to(jnp.arange(TOK_DEV, dtype=jnp.int32)[None, :], (blocks, TOK_DEV))
    taken_mask = (positions < block_counts[:, None]).astype(jnp.int32)
    block_rows = jnp.broadcast_to(jnp.arange(blocks, dtype=jnp.int32)[:, None], (blocks, TOK_DEV))
    chosen_flags = jnp.zeros((blocks, TOK_DEV), jnp.int32).at[block_rows, ranking].set(taken_mask)
    sort_scores = (1 - chosen_flags.reshape(-1)) * TOKENS + jnp.arange(TOKENS, dtype=jnp.int32)
    picked = jnp.argsort(sort_scores, stable=True)[:CAP]
    shuffle = jax.random.permutation(key_shuffle, CAP)
    return picked[shuffle].astype(jnp.int32)


def draw_selections(key, part):
    expert_keys = jax.random.split(jax.random.fold_in(key, 11), SECTIONS * BATCHES * EXPERTS)
    selected = jax.vmap(choose_tokens)(expert_keys)
    return selected.reshape(SECTIONS, BATCHES, EXPERTS, CAP).astype(jnp.int32)


def steps_of(rng, shape, pieces, low, top_value):
    factor_of, own = 1.0, jax.random.fold_in(rng, 6)
    for position, parts in pieces:
        heights = jnp.exp(jax.random.uniform(jax.random.fold_in(own, position), (parts,), jnp.float32, low / len(pieces), top_value / len(pieces)))
        factor_of = factor_of * jnp.repeat(heights, shape[position] // parts).reshape([-1 if axis == position else 1 for axis in range(len(shape))])
    return factor_of


def centred(key, shape, width, limit, cuts=(), kind=jnp.bfloat16):
    loudness = steps_of(key, shape, cuts, -0.22, 0.18) if cuts else 1.0
    entries = jax.random.normal(key, shape, jnp.float32) * width * loudness
    return jnp.minimum(jnp.maximum(entries, -limit), limit).astype(kind)


def setup_inputs(seed: int = 0) -> dict:
    arg_keys = jax.random.split(jax.random.key(seed), 8)
    layer_input = centred(arg_keys[0], (SECTIONS, BATCHES, TOKENS, D), 1.0, 6.0, ((0, 2), (1, 2), (2, 64)))
    grad_output = centred(arg_keys[1], (SECTIONS, BATCHES, TOKENS, D), 0.5, 3.0, ((0, 2), (1, 2), (2, 64)))
    selections = draw_selections(jax.random.fold_in(arg_keys[7], 71), 0)
    gate_values = jnp.clip(jnp.exp(math.log(1.0) - 2.3025851 * jax.random.uniform(arg_keys[3], (SECTIONS, BATCHES, EXPERTS, CAP), jnp.float32) ** steps_of(arg_keys[3], (SECTIONS, BATCHES, EXPERTS, CAP), ((0, 2), (1, 2)), -0.2, 0.2)), 0.1, 1.0)
    gate_weight = centred(arg_keys[4], (SECTIONS, EXPERTS * SPLIT, D, HID_DEV), D ** -0.5, 0.125, ((0, 2), (1, 64), (2, 2)))
    up_weight = centred(arg_keys[5], (SECTIONS, EXPERTS * SPLIT, D, HID_DEV), D ** -0.5, 0.125, ((0, 2), (1, 64), (2, 2)))
    down_weight = centred(arg_keys[6], (SECTIONS, EXPERTS * SPLIT, HID_DEV, D), HID ** -0.5, 0.1875, ((0, 2), (1, 64), (3, 2)))
    return dict(layer_input=layer_input, grad_output=grad_output, selections=selections, gate_values=gate_values, gate_weight=gate_weight, up_weight=up_weight, down_weight=down_weight)


def slice_backward(rows_in, rows_grad, gate_rows, gate_piece, up_piece, down_piece):
    gate_pre = jnp.dot(rows_in, gate_piece, preferred_element_type=jnp.float32)
    up_pre = jnp.dot(rows_in, up_piece, preferred_element_type=jnp.float32)
    sigmoid_gate = jax.nn.sigmoid(gate_pre)
    swish_gate = gate_pre * sigmoid_gate
    activation = (swish_gate * up_pre).astype(jnp.bfloat16)
    upstream = jnp.dot(rows_grad, down_piece.T, preferred_element_type=jnp.float32)
    gate_part = jnp.sum(activation.astype(jnp.float32) * upstream, axis=1)
    scaled = gate_rows[:, None] * upstream
    grad_gate_pre = (scaled * up_pre * sigmoid_gate * (1.0 + gate_pre * (1.0 - sigmoid_gate))).astype(jnp.bfloat16)
    grad_up_pre = (scaled * swish_gate).astype(jnp.bfloat16)
    gated_grad = (gate_rows[:, None] * rows_grad.astype(jnp.float32)).astype(jnp.bfloat16)
    input_part = (jnp.dot(grad_gate_pre, gate_piece.T, preferred_element_type=jnp.float32)
                  + jnp.dot(grad_up_pre, up_piece.T, preferred_element_type=jnp.float32)).astype(jnp.bfloat16)
    gate_term = jnp.dot(rows_in.T, grad_gate_pre, preferred_element_type=jnp.float32).astype(jnp.bfloat16)
    up_term = jnp.dot(rows_in.T, grad_up_pre, preferred_element_type=jnp.float32).astype(jnp.bfloat16)
    down_term = jnp.dot(activation.T, gated_grad, preferred_element_type=jnp.float32).astype(jnp.bfloat16)
    return gate_part, input_part, gate_term, up_term, down_term


def one_batch(layer_rows, grad_rows, chosen, gate_table, gate_all, up_all, down_all):
    branch = jnp.zeros((TOKENS, D), jnp.float32)
    gate_list = []
    gate_terms = []
    up_terms = []
    down_terms = []
    for expert_id in range(EXPERTS):
        picked = chosen[expert_id].astype(jnp.int32)
        rows_in = layer_rows[picked]
        rows_grad = grad_rows[picked]
        gate_total = jnp.zeros((CAP,), jnp.float32)
        for piece_id in range(SPLIT):
            entry = expert_id * SPLIT + piece_id
            results = slice_backward(rows_in, rows_grad, gate_table[expert_id], gate_all[entry], up_all[entry], down_all[entry])
            gate_total = gate_total + results[0]
            branch = branch.at[picked].add(results[1].astype(jnp.float32))
            gate_terms.append(results[2])
            up_terms.append(results[3])
            down_terms.append(results[4])
        gate_list.append(gate_total)
    return (jnp.stack(gate_list), branch.astype(jnp.bfloat16), jnp.stack(gate_terms),
            jnp.stack(up_terms), jnp.stack(down_terms))


def reference(layer_input, grad_output, selections, gate_values, gate_weight, up_weight, down_weight):
    gate_grads = []
    branches = []
    gate_means = []
    up_means = []
    down_means = []
    for segment_id in range(SECTIONS):
        gate_all = gate_weight[segment_id]
        up_all = up_weight[segment_id]
        down_all = down_weight[segment_id]

        def per_batch(batch_items):
            return one_batch(batch_items[0], batch_items[1], batch_items[2], batch_items[3], gate_all, up_all, down_all)

        results = lax.map(per_batch, (layer_input[segment_id], grad_output[segment_id], selections[segment_id], gate_values[segment_id]))
        gate_grads.append(results[0])
        branches.append(results[1])
        gate_means.append(jnp.sum(results[2].astype(jnp.float32), axis=0) / BATCHES)
        up_means.append(jnp.sum(results[3].astype(jnp.float32), axis=0) / BATCHES)
        down_means.append(jnp.sum(results[4].astype(jnp.float32), axis=0) / BATCHES)
    shifted = jnp.concatenate([jnp.stack(branches[1:]), jnp.zeros((1, BATCHES, TOKENS, D), jnp.bfloat16)], axis=0)
    return (shifted, jnp.stack(gate_grads), jnp.stack(gate_means), jnp.stack(up_means), jnp.stack(down_means))
```

```python
import jax
import jax.numpy as jnp
from jax import lax
from jax.experimental import pallas as pl
from jax.experimental.pallas import tpu as pltpu
from jax.sharding import PartitionSpec as P

MESH = pl.DeviceIdType.MESH
BF16 = jnp.bfloat16
F32 = jnp.float32

TOK = 128
WIDTH = 2048
QUARTER = 512
HIDDEN = 256
RANKS = 64
MSG = 16
CAP = 512
HALF = 1024


def dot(left, right):
    return lax.dot_general(left, right, (((1,), (0,)), ((), ())), preferred_element_type=F32)


def dot_last(left, right):
    return lax.dot_general(left, right, (((1,), (1,)), ((), ())), preferred_element_type=F32)


def dot_first(left, right):
    return lax.dot_general(left, right, (((0,), (0,)), ((), ())), preferred_element_type=F32)


def iota(shape, dim):
    return lax.broadcasted_iota(jnp.int32, shape, dim)


def ones_if(condition):
    return jnp.where(condition, 1.0, 0.0).astype(BF16)


def rows_at(index, size):
    return pl.ds(pl.multiple_of(index * size, size), size)


def flip(rank):
    return rank + 1 - 2 * (rank % 2)


def token_selector(sel, block, pair):
    bound = block * TOK + iota((TOK, CAP), 0)
    first = sel[pl.ds(2 * pair, 1), :]
    second = sel[pl.ds(2 * pair + 1, 1), :]
    below = jnp.concatenate([ones_if(first < bound), ones_if(second < bound)], axis=1)
    same = jnp.concatenate([ones_if(first == bound), ones_if(second == bound)], axis=1)
    halves = ones_if((iota((2 * CAP, TOK), 0) < CAP) == (iota((2 * CAP, TOK), 1) < 64))
    rank = dot(below, halves).astype(jnp.int32)
    taken = dot(same, halves)
    start = rank[0:1, :]
    lane = iota((TOK, TOK), 1) & 63
    hit = (taken > 0.5) & ((rank & 3) == (lane >> 4)) & (((rank - start) >> 2) == (lane & 3))
    return jnp.where(hit, 1.0, 0.0)


def slot_selector(mine, member, part):
    row = part * TOK + iota((TOK, CAP), 0)
    bound = (row >> 4) * TOK
    ones = jnp.ones((CAP, TOK), F32).astype(BF16)
    before = dot(ones_if(mine < bound), ones).astype(jnp.int32)
    after = dot(ones_if(mine < bound + TOK), ones).astype(jnp.int32)
    slot = iota((TOK, TOK), 0) & 3
    index = 4 * slot + ((member + 1024 - before) & 3)
    hit = (index < after - before) & (((before + index) >> 2) == iota((TOK, TOK), 1))
    return jnp.where(hit, 1.0, 0.0)


def quarter_of_row(quarter, rows, lanes):
    return ones_if(((iota((rows, lanes), 0) >> 2) & 3) == quarter)


def quarter_of_lane(quarter, rows, lanes):
    return ones_if(((iota((rows, lanes), 1) >> 2) & 3) == quarter)


def spread_rows(selector, source, target):
    def step(i, carry):
        chosen = selector[rows_at(i, 256), :]
        total = None
        for quarter in range(4):
            term = dot(
                chosen * quarter_of_row(quarter, 256, TOK),
                source[:, quarter * QUARTER : (quarter + 1) * QUARTER],
            )
            total = term if total is None else total + term
        target[rows_at(i, 256), :] = total.astype(BF16)
        return carry

    lax.fori_loop(0, 4, step, 0)


def kernel(
    rows,
    grads,
    sel,
    gates,
    gate_w,
    up_w,
    down_w,
    incoming,
    gate_grad,
    gate_wg,
    up_wg,
    down_wg,
    send_rows,
    send_grads,
    recv_rows,
    recv_grads,
    send_back,
    recv_back,
    rows_all,
    grads_all,
    gated_all,
    gate_full,
    up_full,
    down_full,
    gate_pre,
    up_pre,
    act_all,
    ggp_all,
    gup_all,
    to_slot,
    from_token,
    place_of,
    place_from,
    gate_col,
    part_col,
    place_mat,
    part_own,
    part_send,
    part_recv,
    summed,
    term_gate,
    term_up,
    term_down,
    send_tgate,
    send_tup,
    send_tdown,
    recv_tgate,
    recv_tup,
    recv_tdown,
    gsend,
    grecv,
    gsum,
    gall,
    combined,
    arrived,
    s_a2a,
    r_a2a,
    s_w,
    r_w,
    s_rows,
    r_rows,
    s_grads,
    r_grads,
    s_part,
    r_part,
    s_term,
    r_term,
    s_gate,
    r_gate,
    s_spread,
    r_spread,
    s_fin,
    r_fin,
):
    section = lax.axis_index("section")
    me = lax.axis_index("expert")
    dp = lax.axis_index("dp")
    plane = me // 8
    spot = me % 8
    owner = me // 4
    member = me % 4
    mx = flip(member)
    my = (member + 2) % 4
    md = flip(my)
    base = owner * 4
    near_x = base + mx
    near_y = base + my
    far = base + md
    mirror = flip(me)

    barrier = pltpu.get_barrier_semaphore()

    def greet(i, carry):
        pl.semaphore_signal(
            barrier, inc=1, device_id={"expert": (me + i) % RANKS}, device_id_type=MESH
        )
        return carry

    lax.fori_loop(1, RANKS, greet, 0)
    pl.semaphore_signal(barrier, inc=1, device_id={"dp": 1 - dp}, device_id_type=MESH)
    pl.semaphore_signal(
        barrier, inc=1, device_id={"section": 1 - section, "expert": mirror}, device_id_type=MESH
    )

    def make_to_slot(pair, carry):
        tile = token_selector(sel, me, pair)
        to_slot[rows_at(pair, TOK), :] = jnp.transpose(tile).astype(BF16)
        return carry

    lax.fori_loop(0, 8, make_to_slot, 0)
    spread_rows(to_slot, rows, send_rows)

    pl.semaphore_wait(barrier, RANKS + 1)

    def remote(source, target, s_sem, r_sem, where):
        return pltpu.make_async_remote_copy(
            src_ref=source,
            dst_ref=target,
            send_sem=s_sem,
            recv_sem=r_sem,
            device_id=where,
            device_id_type=MESH,
        )

    def exchange(source, target, index, mirrored):
        def step(i, carry):
            turn = i % 8
            dz = (turn % 2) * ((turn + 1) // 2) + (1 - turn % 2) * ((8 - turn // 2) % 8)
            to = ((plane + dz) % 8) * 8 + (spot + i // 8) % 8
            block = flip(to) if mirrored else to
            remote(
                source.at[rows_at(block, MSG)],
                target.at[rows_at(me, MSG)],
                s_a2a.at[index],
                r_a2a.at[index],
                {"expert": to},
            ).start()
            return carry

        lax.fori_loop(1, RANKS, step, 0)
        block = flip(me) if mirrored else me
        target[rows_at(me, MSG), :] = source[rows_at(block, MSG), :]

    def drain(ref, sem):
        view = ref.at[pl.ds(0, (RANKS - 1) * MSG)]
        pltpu.make_async_copy(view, view, sem).wait()

    def await_copy(view, sem):
        pltpu.make_async_copy(view, view, sem).wait()

    exchange(send_rows, recv_rows, 0, False)

    partner = {"dp": 1 - dp}
    weight_copies = [
        remote(gate_w, gate_full.at[rows_at(dp, HALF)], s_w.at[0], r_w.at[0], partner),
        remote(up_w, up_full.at[rows_at(dp, HALF)], s_w.at[1], r_w.at[1], partner),
        remote(down_w, down_full.at[dp], s_w.at[2], r_w.at[2], partner),
    ]
    for copy in weight_copies:
        copy.start()

    spread_rows(to_slot, grads, send_grads)
    exchange(send_grads, recv_grads, 1, False)

    gate_full[rows_at(dp, HALF), :] = gate_w[...]
    up_full[rows_at(dp, HALF), :] = up_w[...]
    down_full[dp] = down_w[...]

    mine = sel[pl.ds(owner, 1), :]

    def make_place(part, carry):
        tile = slot_selector(mine, member, part)
        place_of[rows_at(part, TOK), :] = tile.astype(BF16)
        place_from[:, rows_at(part, TOK)] = jnp.transpose(tile).astype(BF16)
        return carry

    lax.fori_loop(0, 8, make_place, 0)

    def make_from_token(pair, carry):
        from_token[:, rows_at(pair, TOK)] = token_selector(sel, mirror, pair).astype(BF16)
        return carry

    lax.fori_loop(0, 8, make_from_token, 0)

    across = iota((CAP, CAP), 1)
    down = iota((CAP, CAP), 0)
    mine_f = mine.astype(F32)
    mine_col = jnp.sum(jnp.where(across == down, mine_f, 0.0), axis=1, keepdims=True)
    rank = jnp.sum(jnp.where(mine_col < mine_f, 1.0, 0.0), axis=0, keepdims=True).astype(jnp.int32)
    place = (rank & 3) * TOK + (rank >> 2)
    place_mat[...] = jnp.where(place == down, 1.0, 0.0)
    gate_col[...] = jnp.sum(
        jnp.where(place_mat[...] > 0.5, gates[pl.ds(owner, 1), :], 0.0), axis=1, keepdims=True
    )

    def compact(source, target):
        view = target.at[rows_at(member, TOK)]
        for quarter in range(4):
            chosen = place_from[...] * quarter_of_lane(quarter, TOK, RANKS * MSG)
            view[:, quarter * QUARTER : (quarter + 1) * QUARTER] = dot(chosen, source[...]).astype(
                BF16
            )

    low, high = pl.ds(0, HALF), pl.ds(HALF, HALF)

    def gather_own(ref, s, r):
        own = ref.at[rows_at(member, TOK)]
        remote(own, own, s.at[0], r.at[0], {"expert": near_x}).start()
        remote(own, own, s.at[1], r.at[1], {"expert": near_y}).start()

    def gather_forward(ref, s, r):
        from_x = ref.at[rows_at(mx, TOK)]
        await_copy(from_x, r.at[0])
        view = ref.at[rows_at(mx, TOK), low]
        remote(view, view, s.at[2], r.at[2], {"expert": near_y}).start()
        from_y = ref.at[rows_at(my, TOK)]
        await_copy(from_y, r.at[1])
        view = ref.at[rows_at(my, TOK), high]
        remote(view, view, s.at[3], r.at[3], {"expert": near_x}).start()

    def gather_far(ref, r):
        await_copy(ref.at[rows_at(md, TOK), low], r.at[2])
        await_copy(ref.at[rows_at(md, TOK), high], r.at[3])

    def gather_sent(ref, s):
        await_copy(ref.at[rows_at(member, TOK)], s.at[0])
        await_copy(ref.at[rows_at(member, TOK)], s.at[1])
        await_copy(ref.at[rows_at(mx, TOK), low], s.at[2])
        await_copy(ref.at[rows_at(my, TOK), high], s.at[3])

    def forward(block):
        at = rows_at(block, TOK)
        gate_pre[at, :] = dot(rows_all[at, :], gate_full[...])
        up_pre[at, :] = dot(rows_all[at, :], up_full[...])

    def backward(block):
        at = rows_at(block, TOK)
        grad = grads_all[at, :]
        upstream = dot_last(grad[:, :HALF], down_full[0]) + dot_last(grad[:, HALF:], down_full[1])
        pre, up = gate_pre[at, :], up_pre[at, :]
        sigmoid = jax.nn.sigmoid(pre)
        swish = pre * sigmoid
        activation = (swish * up).astype(BF16)
        gate = gate_col[at, :]
        part_col[at, :] = jnp.sum(activation.astype(F32) * upstream, axis=1, keepdims=True)
        scaled = gate * upstream
        ggp = (scaled * up * sigmoid * (1.0 + pre * (1.0 - sigmoid))).astype(BF16)
        gup = (scaled * swish).astype(BF16)
        act_all[at, :] = activation
        ggp_all[at, :] = ggp
        gup_all[at, :] = gup
        gated_all[at, :] = (gate * grad.astype(F32)).astype(BF16)
        return dot_last(ggp, gate_full[...]) + dot_last(gup, up_full[...])

    drain(recv_rows, r_a2a.at[0])
    compact(recv_rows, rows_all)
    gather_own(rows_all, s_rows, r_rows)
    for i, view in enumerate(
        (gate_full.at[rows_at(1 - dp, HALF)], up_full.at[rows_at(1 - dp, HALF)], down_full.at[1 - dp])
    ):
        await_copy(view, r_w.at[i])
    forward(member)
    gather_forward(rows_all, s_rows, r_rows)
    forward(mx)
    forward(my)
    gather_far(rows_all, r_rows)
    forward(md)

    drain(recv_grads, r_a2a.at[1])
    compact(recv_grads, grads_all)
    gather_own(grads_all, s_grads, r_grads)
    part_own[...] = backward(member)
    gather_forward(grads_all, s_grads, r_grads)
    part_copies = [
        remote(part_send.at[i], part_recv.at[i], s_part.at[i], r_part.at[i], {"expert": to})
        for i, to in enumerate((near_x, near_y, far))
    ]
    part_send[0] = backward(mx).astype(BF16)
    part_copies[0].start()
    part_send[1] = backward(my).astype(BF16)
    part_copies[1].start()
    gather_far(grads_all, r_grads)
    part_send[2] = backward(md).astype(BF16)
    part_copies[2].start()

    part_row = jnp.sum(place_mat[...] * part_col[...], axis=0, keepdims=True)
    gsend[...] = jnp.zeros((8, TOK), F32)
    for i in range(4):
        gsend[i : i + 1, :] = part_row[:, i * TOK : (i + 1) * TOK]
    gate_copies = [
        remote(gsend, grecv.at[i], s_gate.at[i], r_gate.at[i], {"expert": to})
        for i, to in enumerate((near_x, near_y, far))
    ]
    for copy in gate_copies:
        copy.start()

    def weight_terms(half, gate_to, up_to, down_to):
        def step(i, carry):
            columns = pl.ds(pl.multiple_of(half * HALF + i * 256, 256), 256)
            left = rows_all[:, columns]
            gate_to[rows_at(i, 256), :] = dot_first(left, ggp_all[...]).astype(BF16)
            up_to[rows_at(i, 256), :] = dot_first(left, gup_all[...]).astype(BF16)
            down_to[:, rows_at(i, 256)] = dot_first(act_all[...], gated_all[:, columns]).astype(BF16)
            return carry

        lax.fori_loop(0, 4, step, 0)

    weight_terms(1 - dp, send_tgate, send_tup, send_tdown)
    term_copies = [
        remote(send_tgate, recv_tgate, s_term.at[0], r_term.at[0], partner),
        remote(send_tup, recv_tup, s_term.at[1], r_term.at[1], partner),
        remote(send_tdown, recv_tdown, s_term.at[2], r_term.at[2], partner),
    ]
    for copy in term_copies:
        copy.start()

    for copy in gate_copies:
        copy.wait_recv()
    gsum[...] = (gsend[...] + grecv[0]) + (grecv[1] + grecv[2])

    def spread_gate(i, carry):
        to = ((owner + i) % 16) * 4 + member
        remote(gsum, gall.at[rows_at(owner, 8)], s_spread, r_spread, {"expert": to}).start()
        return carry

    lax.fori_loop(1, 16, spread_gate, 0)
    gall[rows_at(owner, 8), :] = gsum[...]

    weight_terms(dp, term_gate, term_up, term_down)

    for copy in part_copies:
        copy.wait_recv()
    summed[...] = (
        (part_own[...] + part_recv[0].astype(F32))
        + (part_recv[1].astype(F32) + part_recv[2].astype(F32))
    ).astype(BF16)
    spread_rows(place_of, summed, send_back)
    exchange(send_back, recv_back, 2, True)

    for copy in term_copies:
        copy.wait_recv()
    gate_wg[...] = (term_gate[...].astype(F32) + recv_tgate[...].astype(F32)) * 0.5
    up_wg[...] = (term_up[...].astype(F32) + recv_tup[...].astype(F32)) * 0.5
    down_wg[...] = (term_down[...].astype(F32) + recv_tdown[...].astype(F32)) * 0.5

    others = gall.at[pl.ds(0, 15 * 8)]
    await_copy(others, r_spread)
    for e in range(16):
        for i in range(4):
            gate_grad[e : e + 1, i * TOK : (i + 1) * TOK] = gall[e * 8 + i : e * 8 + i + 1, :]

    drain(recv_back, r_a2a.at[2])
    for quarter in range(4):
        chosen = from_token[...] * quarter_of_lane(quarter, TOK, RANKS * MSG)
        combined[:, quarter * QUARTER : (quarter + 1) * QUARTER] = dot(
            chosen, recv_back[...]
        ).astype(BF16)
    last = remote(combined, arrived, s_fin, r_fin, {"section": 0, "expert": mirror})

    @pl.when(section == 1)
    def _():
        last.start()
        incoming[...] = jnp.zeros((TOK, WIDTH), BF16)
        last.wait_send()

    @pl.when(section == 0)
    def _():
        last.wait_recv()
        incoming[...] = arrived[...]

    drain(send_rows, s_a2a.at[0])
    drain(send_grads, s_a2a.at[1])
    drain(send_back, s_a2a.at[2])
    for copy in (*weight_copies, *part_copies, *gate_copies, *term_copies):
        copy.wait_send()
    gather_sent(rows_all, s_rows)
    gather_sent(grads_all, s_grads)
    await_copy(others, s_spread)


def on_device(
    layer_input, grad_output, selections, gate_values, gate_weight, up_weight, down_weight
):
    vmem = pl.BlockSpec(memory_space=pltpu.VMEM)
    shape = jax.ShapeDtypeStruct
    dma = pltpu.SemaphoreType.DMA
    message = pltpu.VMEM((RANKS * MSG, QUARTER), BF16)
    wide = pltpu.VMEM((CAP, WIDTH), BF16)
    pre = pltpu.VMEM((CAP, HIDDEN), F32)
    post = pltpu.VMEM((CAP, HIDDEN), BF16)
    tall = pltpu.VMEM((RANKS * MSG, TOK), BF16)
    flat = pltpu.VMEM((TOK, RANKS * MSG), BF16)
    tile = pltpu.VMEM((HALF, HIDDEN), BF16)
    tile_t = pltpu.VMEM((HIDDEN, HALF), BF16)
    outs = pl.pallas_call(
        kernel,
        out_shape=(
            shape((TOK, WIDTH), BF16),
            shape((16, CAP), F32),
            shape((HALF, HIDDEN), F32),
            shape((HALF, HIDDEN), F32),
            shape((HIDDEN, HALF), F32),
        ),
        in_specs=[vmem] * 7,
        out_specs=(vmem,) * 5,
        scratch_shapes=[
            message,
            message,
            message,
            message,
            message,
            message,
            wide,
            wide,
            wide,
            pltpu.VMEM((WIDTH, HIDDEN), BF16),
            pltpu.VMEM((WIDTH, HIDDEN), BF16),
            pltpu.VMEM((2, HIDDEN, HALF), BF16),
            pre,
            pre,
            post,
            post,
            post,
            tall,
            flat,
            tall,
            flat,
            pltpu.VMEM((CAP, 1), F32),
            pltpu.VMEM((CAP, 1), F32),
            pltpu.VMEM((CAP, CAP), F32),
            pltpu.VMEM((TOK, WIDTH), F32),
            pltpu.VMEM((3, TOK, WIDTH), BF16),
            pltpu.VMEM((3, TOK, WIDTH), BF16),
            pltpu.VMEM((TOK, WIDTH), BF16),
            tile,
            tile,
            tile_t,
            tile,
            tile,
            tile_t,
            tile,
            tile,
            tile_t,
            pltpu.VMEM((8, TOK), F32),
            pltpu.VMEM((3, 8, TOK), F32),
            pltpu.VMEM((8, TOK), F32),
            pltpu.VMEM((16 * 8, TOK), F32),
            pltpu.VMEM((TOK, WIDTH), BF16),
            pltpu.VMEM((TOK, WIDTH), BF16),
            dma((3,)),
            dma((3,)),
            dma((3,)),
            dma((3,)),
            dma((4,)),
            dma((4,)),
            dma((4,)),
            dma((4,)),
            dma((3,)),
            dma((3,)),
            dma((3,)),
            dma((3,)),
            dma((3,)),
            dma((3,)),
            dma,
            dma,
            dma,
            dma,
        ],
        compiler_params=pltpu.CompilerParams(
            collective_id=0, has_side_effects=True, vmem_limit_bytes=56 * 2**20
        ),
        cost_estimate=pl.CostEstimate(
            flops=8_000_000_000, bytes_accessed=8_000_000, transcendentals=131072
        ),
    )(
        layer_input[0, 0],
        grad_output[0, 0],
        selections[0, 0],
        gate_values[0, 0],
        gate_weight[0, 0],
        up_weight[0, 0],
        down_weight[0, 0],
    )
    return tuple(out[None, None] for out in outs)


def solution(mesh):
    return jax.shard_map(
        on_device,
        mesh=mesh,
        in_specs=(
            P("section", "dp", "expert", None),
            P("section", "dp", "expert", None),
            P("section", "dp", None, None),
            P("section", "dp", None, None),
            P("section", "expert", "dp", None),
            P("section", "expert", "dp", None),
            P("section", "expert", None, "dp"),
        ),
        out_specs=(
            P("section", "dp", "expert", None),
            P("section", "dp", None, None),
            P("section", "expert", "dp", None),
            P("section", "expert", "dp", None),
            P("section", "expert", None, "dp"),
        ),
        check_vma=False,
    )
```

```python
import jax
import jax.numpy as jnp
from jax import lax
from jax.experimental import pallas as pl
from jax.experimental.pallas import tpu as pltpu
from jax.sharding import PartitionSpec as P

MESH = pl.DeviceIdType.MESH
BF16 = jnp.bfloat16
F32 = jnp.float32

TOK = 128
WIDTH = 2048
HIDDEN = 256
RANKS = 64
MSG = 16
ALL = RANKS * MSG
CAP = 512
HALF = 1024
PIECES = 4
PIECE = WIDTH // PIECES


def dot(left, right):
    return lax.dot_general(left, right, (((1,), (0,)), ((), ())), preferred_element_type=F32)


def dot_last(left, right):
    return lax.dot_general(left, right, (((1,), (1,)), ((), ())), preferred_element_type=F32)


def dot_first(left, right):
    return lax.dot_general(left, right, (((0,), (0,)), ((), ())), preferred_element_type=F32)


def iota(shape, dim):
    return lax.broadcasted_iota(jnp.int32, shape, dim)


def one_if(condition):
    return jnp.where(condition, 1.0, 0.0)


def ones_if(condition):
    return one_if(condition).astype(BF16)


def rows_at(index, size):
    return pl.ds(pl.multiple_of(index * size, size), size)


def flip(rank):
    return rank + 1 - 2 * (rank % 2)


def slot_codes(sel, columns, block):
    tokens = (block * TOK + iota((CAP, TOK), 1)).astype(F32)
    taken = jnp.concatenate(
        [
            jnp.sum(one_if(columns[:, e : e + 1] == tokens), axis=0, keepdims=True)
            for e in range(16)
        ],
        axis=0,
    )
    upper = ones_if(iota((TOK, TOK), 0) < iota((TOK, TOK), 1))
    index = dot(taken.astype(BF16), upper).astype(jnp.int32)
    start = jnp.sum(one_if(sel < block * TOK), axis=1, keepdims=True).astype(jnp.int32)
    return jnp.where(taken > 0.5, ((start + index) & 3) * 16 + (index >> 2), -1)


def slot_selector(mine, member, part):
    row = part * TOK + iota((TOK, CAP), 0)
    bound = (row >> 4) * TOK
    ones = jnp.ones((CAP, TOK), F32).astype(BF16)
    before = dot(ones_if(mine < bound), ones).astype(jnp.int32)
    after = dot(ones_if(mine < bound + TOK), ones).astype(jnp.int32)
    slot = iota((TOK, TOK), 0) & 3
    index = 4 * slot + ((member + 1024 - before) & 3)
    hit = (index < after - before) & (((before + index) >> 2) == iota((TOK, TOK), 1))
    return one_if(hit)


def quarter(shape, dim, which):
    return ((iota(shape, dim) >> 2) & 3) == which


def spread_rows(selector, source, start, width, target):
    part = width // 4

    def step(i, carry):
        stacked = jnp.concatenate(
            [source[:, start + s * part : start + (s + 1) * part] for s in range(4)], axis=0
        )
        target[rows_at(i, 256), :] = dot(selector[rows_at(i, 256), :], stacked).astype(BF16)
        return carry

    lax.fori_loop(0, 4, step, 0)


def kernel(
    rows,
    grads,
    sel,
    gates,
    gate_w,
    up_w,
    down_w,
    incoming,
    gate_grad,
    gu_own,
    gu_other,
    down_own,
    down_other,
    send_fwd,
    recv_fwd,
    send_back,
    recv_back,
    rows_all,
    grads_all,
    gated_all,
    gu_full,
    down_full,
    pre_all,
    ups_all,
    act_all,
    act_t,
    gg_all,
    codes,
    to_slot,
    from_token,
    place_of,
    place_from,
    gate_col,
    part_col,
    place_mat,
    part_own,
    part_send,
    part_recv,
    summed,
    gu_send,
    gu_keep,
    down_send,
    down_keep,
    gsend,
    grecv,
    gsum,
    gall,
    combined,
    arrived,
    s_fwd,
    r_fwd,
    s_back,
    r_back,
    s_w,
    r_w,
    s_own,
    s_gather,
    r_gather,
    s_part,
    r_part,
    s_term,
    r_term,
    s_out,
    s_gate,
    r_gate,
    s_spread,
    r_spread,
    s_fin,
    r_fin,
):
    section = lax.axis_index("section")
    me = lax.axis_index("expert")
    dp = lax.axis_index("dp")
    plane = me // 8
    spot = me % 8
    owner = me // 4
    member = me % 4
    mx = flip(member)
    my = (member + 2) % 4
    md = flip(my)
    near_x = owner * 4 + mx
    near_y = owner * 4 + my
    far = owner * 4 + md
    mirror = flip(me)

    def remote(source, target, s_sem, r_sem, where):
        return pltpu.make_async_remote_copy(
            src_ref=source,
            dst_ref=target,
            send_sem=s_sem,
            recv_sem=r_sem,
            device_id=where,
            device_id_type=MESH,
        )

    def await_copy(view, sem):
        pltpu.make_async_copy(view, view, sem).wait()

    barrier = pltpu.get_barrier_semaphore()

    def greet(i, carry):
        pl.semaphore_signal(
            barrier, inc=1, device_id={"expert": (me + i) % RANKS}, device_id_type=MESH
        )
        return carry

    lax.fori_loop(1, RANKS, greet, 0)
    pl.semaphore_signal(barrier, inc=1, device_id={"dp": 1 - dp}, device_id_type=MESH)
    pl.semaphore_signal(
        barrier, inc=1, device_id={"section": 1 - section, "expert": mirror}, device_id_type=MESH
    )

    gate_cols, up_cols = pl.ds(0, HIDDEN), pl.ds(HIDDEN, HIDDEN)
    weight_views = [
        (gate_w, gu_full.at[rows_at(dp, HALF), gate_cols]),
        (up_w, gu_full.at[rows_at(dp, HALF), up_cols]),
        (down_w, down_full.at[dp]),
    ]
    own_copies = [
        pltpu.make_async_copy(source, target, s_own.at[i])
        for i, (source, target) in enumerate(weight_views)
    ]
    for copy in own_copies:
        copy.start()

    columns = jnp.transpose(sel[...].astype(F32))
    codes[...] = slot_codes(sel[...], columns, me)

    def make_to_slot(e, carry):
        line = iota((64, TOK), 0)
        hit = codes[pl.ds(e, 1), :] == line - (line & 12)
        for s in range(4):
            to_slot[rows_at(e, 64), s * TOK : (s + 1) * TOK] = ones_if(
                hit & quarter((64, TOK), 0, s)
            )
        return carry

    lax.fori_loop(0, 16, make_to_slot, 0)
    spread_rows(to_slot, rows, 0, HALF, send_fwd.at[0])

    pl.semaphore_wait(barrier, RANKS + 1)

    planes = [((plane + dz) % 8) * 8 for dz in (4, 1, 7, 2, 6, 3, 5, 0)]

    def exchange(source, target, s_sem, r_sem, mirrored):
        def send(to):
            block = flip(to) if mirrored else to
            remote(
                source.at[rows_at(block, MSG)],
                target.at[rows_at(me, MSG)],
                s_sem,
                r_sem,
                {"expert": to},
            ).start()

        def step(i, carry):
            place = (spot + i) % 8
            for start in planes:
                send(start + place)
            return carry

        for start in planes[:-1]:
            send(start + spot)
        lax.fori_loop(1, 8, step, 0)
        block = flip(me) if mirrored else me
        target[rows_at(me, MSG), :] = source[rows_at(block, MSG), :]

    def drain(ref, sem):
        await_copy(ref.at[pl.ds(0, (RANKS - 1) * MSG)], sem)

    def dispatch(i):
        exchange(send_fwd.at[i], recv_fwd.at[i], s_fwd.at[i], r_fwd.at[i], False)

    dispatch(0)
    partner = {"dp": 1 - dp}
    weight_copies = [
        remote(source, target, s_w.at[i], r_w.at[i], partner)
        for i, (source, target) in enumerate(weight_views)
    ]
    for copy in weight_copies:
        copy.start()
    spread_rows(to_slot, rows, HALF, HALF, send_fwd.at[1])
    dispatch(1)
    spread_rows(to_slot, grads, 0, HALF, send_fwd.at[2])
    dispatch(2)
    spread_rows(to_slot, grads, HALF, HALF, send_fwd.at[3])
    dispatch(3)

    mine = sel[pl.ds(owner, 1), :]

    def make_place(part, carry):
        tile = slot_selector(mine, member, part)
        turned = jnp.transpose(tile)
        for s in range(4):
            keep = slice(s * TOK, (s + 1) * TOK)
            place_of[rows_at(part, TOK), keep] = (
                tile * one_if(quarter((TOK, TOK), 0, s))
            ).astype(BF16)
            place_from[keep, rows_at(part, TOK)] = (
                turned * one_if(quarter((TOK, TOK), 1, s))
            ).astype(BF16)
        return carry

    lax.fori_loop(0, 8, make_place, 0)

    def make_tables():
        across = iota((CAP, CAP), 1)
        down = iota((CAP, CAP), 0)
        mine_f = mine.astype(F32)
        mine_col = jnp.sum(jnp.where(across == down, mine_f, 0.0), axis=1, keepdims=True)
        rank = jnp.sum(one_if(mine_col < mine_f), axis=0, keepdims=True).astype(jnp.int32)
        place = (rank & 3) * TOK + (rank >> 2)
        place_mat[...] = one_if(place == down)
        gate_col[...] = jnp.sum(
            jnp.where(place_mat[...] > 0.5, gates[pl.ds(owner, 1), :], 0.0), axis=1, keepdims=True
        )

    def make_from_token():
        codes[...] = slot_codes(sel[...], columns, mirror)

        def step(pair, carry):
            line = iota((TOK, TOK), 0)
            inner = line & 63
            wanted = jnp.where(
                line < 64, codes[pl.ds(2 * pair, 1), :], codes[pl.ds(2 * pair + 1, 1), :]
            )
            turned = jnp.transpose(one_if(wanted == inner - (inner & 12)))
            for s in range(4):
                from_token[s * TOK : (s + 1) * TOK, rows_at(pair, TOK)] = (
                    turned * one_if(quarter((TOK, TOK), 1, s))
                ).astype(BF16)
            return carry

        lax.fori_loop(0, 8, step, 0)

    def whole(i):
        return rows_all if i < 2 else grads_all

    def half_view(i, block, offset, width):
        return whole(i).at[rows_at(block, TOK), pl.ds((i % 2) * HALF + offset, width)]

    def gather_own(i):
        drain(recv_fwd.at[i], r_fwd.at[i])
        compacted = dot(place_from[...], recv_fwd[i])
        for s in range(4):
            start = (i % 2) * HALF + s * 256
            whole(i)[rows_at(member, TOK), start : start + 256] = compacted[
                s * TOK : (s + 1) * TOK, :
            ].astype(BF16)
        own = half_view(i, member, 0, HALF)
        remote(own, own, s_gather.at[i, 0], r_gather.at[i, 0], {"expert": near_x}).start()
        remote(own, own, s_gather.at[i, 1], r_gather.at[i, 1], {"expert": near_y}).start()

    def gather_forward(i):
        await_copy(half_view(i, mx, 0, HALF), r_gather.at[i, 0])
        view = half_view(i, mx, 0, CAP)
        remote(view, view, s_gather.at[i, 2], r_gather.at[i, 2], {"expert": near_y}).start()
        await_copy(half_view(i, my, 0, HALF), r_gather.at[i, 1])
        view = half_view(i, my, CAP, CAP)
        remote(view, view, s_gather.at[i, 3], r_gather.at[i, 3], {"expert": near_x}).start()

    def gather_far(i):
        await_copy(half_view(i, md, 0, CAP), r_gather.at[i, 2])
        await_copy(half_view(i, md, CAP, CAP), r_gather.at[i, 3])

    def gather_sent(i):
        await_copy(half_view(i, member, 0, HALF), s_gather.at[i, 0])
        await_copy(half_view(i, member, 0, HALF), s_gather.at[i, 1])
        await_copy(half_view(i, mx, 0, CAP), s_gather.at[i, 2])
        await_copy(half_view(i, my, CAP, CAP), s_gather.at[i, 3])

    def forward(i, block):
        at = rows_at(block, TOK)
        half = slice(i * HALF, (i + 1) * HALF)
        product = dot(rows_all[at, half], gu_full[half, :])
        pre_all[at, :] = product if i == 0 else pre_all[at, :] + product

    def upstream(i, block):
        at = rows_at(block, TOK)
        grad = grads_all[at, i * HALF : (i + 1) * HALF]
        gated_all[at, i * HALF : (i + 1) * HALF] = (gate_col[at, :] * grad.astype(F32)).astype(BF16)
        product = dot_last(grad, down_full[i])
        ups_all[at, :] = product if i == 0 else ups_all[at, :] + product

    def backward(block):
        at = rows_at(block, TOK)
        ups, pre, up = ups_all[at, :], pre_all[at, :HIDDEN], pre_all[at, HIDDEN:]
        sigmoid = jax.nn.sigmoid(pre)
        swish = pre * sigmoid
        activation = (swish * up).astype(BF16)
        part_col[at, :] = jnp.sum(activation.astype(F32) * ups, axis=1, keepdims=True)
        scaled = gate_col[at, :] * ups
        act_all[at, :] = activation
        gg_all[at, :HIDDEN] = (scaled * up * sigmoid * (1.0 + pre * (1.0 - sigmoid))).astype(BF16)
        gg_all[at, HIDDEN:] = (scaled * swish).astype(BF16)

    def input_part(block, c):
        return dot_last(gg_all[rows_at(block, TOK), :], gu_full[c * PIECE : (c + 1) * PIECE, :])

    roles = ((mx, near_x), (my, near_y), (md, far))

    def part_copy(role, c):
        return remote(
            part_send.at[role, c],
            part_recv.at[role, c],
            s_part.at[role, c],
            r_part.at[role, c],
            {"expert": roles[role][1]},
        )

    def send_part(role, c):
        part_send[role, c] = input_part(roles[role][0], c).astype(BF16)
        part_copy(role, c).start()

    gather_own(0)
    make_tables()
    gather_forward(0)
    for i, (source, target) in enumerate(weight_views):
        await_copy(target, s_own.at[i])
    for i, view in enumerate(
        (
            gu_full.at[rows_at(1 - dp, HALF), gate_cols],
            gu_full.at[rows_at(1 - dp, HALF), up_cols],
            down_full.at[1 - dp],
        )
    ):
        await_copy(view, r_w.at[i])
    gather_own(1)
    for block in (member, mx, my):
        forward(0, block)
    make_from_token()
    gather_far(0)
    gather_forward(1)
    gather_own(2)
    forward(0, md)
    for block in (member, mx, my):
        forward(1, block)
    upstream(0, member)
    gather_far(1)
    gather_forward(2)
    gather_own(3)
    forward(1, md)
    upstream(0, mx)
    upstream(0, my)
    upstream(1, member)
    backward(member)
    for c in range(PIECES):
        part_own[:, c * PIECE : (c + 1) * PIECE] = input_part(member, c)
    gather_far(2)
    upstream(0, md)
    gather_forward(3)
    for role in range(2):
        upstream(1, roles[role][0])
        backward(roles[role][0])
        send_part(role, 0)
    gather_far(3)
    upstream(1, md)
    backward(md)
    send_part(2, 0)
    for c in range(1, PIECES):
        for role in (2, 0, 1):
            send_part(role, c)

    for b in range(4):
        act_t[:, b * TOK : (b + 1) * TOK] = jnp.transpose(
            act_all[b * TOK : (b + 1) * TOK, :].astype(F32)
        ).astype(BF16)

    def weight_terms(half, gu_to, down_to):
        def step(i, carry):
            columns = pl.ds(pl.multiple_of(half * HALF + i * 256, 256), 256)
            gu_to[rows_at(i, 256), :] = dot_first(rows_all[:, columns], gg_all[...]).astype(BF16)
            down_to[:, rows_at(i, 256)] = dot(act_t[...], gated_all[:, columns]).astype(BF16)
            return carry

        lax.fori_loop(0, 4, step, 0)

    weight_terms(1 - dp, gu_send, down_send)
    term_copies = [
        remote(gu_send, gu_other, s_term.at[0], r_term.at[0], partner),
        remote(down_send, down_other, s_term.at[1], r_term.at[1], partner),
    ]
    for copy in term_copies:
        copy.start()

    def give_back(c):
        for role in range(3):
            await_copy(part_recv.at[role, c], r_part.at[role, c])
        summed[...] = (
            (part_own[:, c * PIECE : (c + 1) * PIECE] + part_recv[0, c].astype(F32))
            + (part_recv[1, c].astype(F32) + part_recv[2, c].astype(F32))
        ).astype(BF16)
        spread_rows(place_of, summed, 0, PIECE, send_back.at[c])
        exchange(send_back.at[c], recv_back.at[c], s_back.at[c], r_back.at[c], True)

    def last_copy(c):
        view = pl.ds(c * PIECE, PIECE)
        return remote(
            combined.at[:, view],
            arrived.at[:, view],
            s_fin.at[c],
            r_fin.at[c],
            {"section": 0, "expert": mirror},
        )

    def combine(c):
        drain(recv_back.at[c], r_back.at[c])
        sums = dot(from_token[...], recv_back[c]).astype(BF16)
        part = PIECE // 4
        for s in range(4):
            start = c * PIECE + s * part
            combined[:, start : start + part] = sums[s * TOK : (s + 1) * TOK, :]

        @pl.when(section == 1)
        def _():
            last_copy(c).start()

    give_back(0)

    part_row = jnp.sum(place_mat[...] * part_col[...], axis=0, keepdims=True)
    gsend[...] = jnp.zeros((8, TOK), F32)
    for i in range(4):
        gsend[i : i + 1, :] = part_row[:, i * TOK : (i + 1) * TOK]
    gate_copies = [
        remote(gsend, grecv.at[i], s_gate.at[i], r_gate.at[i], {"expert": to})
        for i, (_, to) in enumerate(roles)
    ]
    for copy in gate_copies:
        copy.start()

    give_back(1)
    weight_terms(dp, gu_keep, down_keep)
    out_copies = [
        pltpu.make_async_copy(gu_keep, gu_own, s_out.at[0]),
        pltpu.make_async_copy(down_keep, down_own, s_out.at[1]),
    ]
    for copy in out_copies:
        copy.start()
    combine(0)
    give_back(2)

    for copy in gate_copies:
        copy.wait_recv()
    gsum[...] = (gsend[...] + grecv[0]) + (grecv[1] + grecv[2])

    def spread_gate(i, carry):
        to = ((owner + i) % 16) * 4 + member
        remote(gsum, gall.at[rows_at(owner, 8)], s_spread, r_spread, {"expert": to}).start()
        return carry

    lax.fori_loop(1, 16, spread_gate, 0)
    gall[rows_at(owner, 8), :] = gsum[...]

    combine(1)
    give_back(3)
    combine(2)

    others = gall.at[pl.ds(0, 15 * 8)]
    await_copy(others, r_spread)
    for e in range(16):
        for i in range(4):
            gate_grad[e : e + 1, i * TOK : (i + 1) * TOK] = gall[e * 8 + i : e * 8 + i + 1, :]

    combine(3)

    for i in range(4):
        drain(send_fwd.at[i], s_fwd.at[i])
        gather_sent(i)
    for c in range(PIECES):
        drain(send_back.at[c], s_back.at[c])
        for role in range(3):
            await_copy(part_send.at[role, c], s_part.at[role, c])
    for copy in (*weight_copies, *gate_copies, *term_copies):
        copy.wait_send()
    await_copy(others, s_spread)
    for copy in term_copies:
        copy.wait_recv()
    for copy in out_copies:
        copy.wait()

    @pl.when(section == 1)
    def _():
        incoming[...] = jnp.zeros((TOK, WIDTH), BF16)
        for c in range(PIECES):
            last_copy(c).wait_send()

    @pl.when(section == 0)
    def _():
        for c in range(PIECES):
            last_copy(c).wait_recv()
            keep = slice(c * PIECE, (c + 1) * PIECE)
            incoming[:, keep] = arrived[:, keep]


def finish(
    incoming, gate_grad, gu_own, gu_other, down_own, down_other, *outs
):
    incoming_to, gate_grad_to, gate_to, up_to, down_to = outs
    incoming_to[...] = incoming[...]
    gate_grad_to[...] = gate_grad[...]
    total = (gu_own[...].astype(F32) + gu_other[...].astype(F32)) * 0.5
    gate_to[...] = total[:, :HIDDEN]
    up_to[...] = total[:, HIDDEN:]
    down_to[...] = (down_own[...].astype(F32) + down_other[...].astype(F32)) * 0.5


def on_device(
    layer_input, grad_output, selections, gate_values, gate_weight, up_weight, down_weight
):
    vmem = pl.BlockSpec(memory_space=pltpu.VMEM)
    hbm = pl.BlockSpec(memory_space=pl.ANY)
    shape = jax.ShapeDtypeStruct
    dma = pltpu.SemaphoreType.DMA

    def held(*dims):
        return pltpu.VMEM(dims, BF16)

    def held32(*dims):
        return pltpu.VMEM(dims, F32)

    part = PIECE // 4
    middle = pl.pallas_call(
        kernel,
        out_shape=(
            shape((TOK, WIDTH), BF16),
            shape((16, CAP), F32),
            shape((HALF, 2 * HIDDEN), BF16),
            shape((HALF, 2 * HIDDEN), BF16),
            shape((HIDDEN, HALF), BF16),
            shape((HIDDEN, HALF), BF16),
        ),
        in_specs=[vmem] * 4 + [hbm] * 3,
        out_specs=(vmem, vmem, hbm, hbm, hbm, hbm),
        scratch_shapes=[
            held(4, ALL, 256),
            held(4, ALL, 256),
            held(PIECES, ALL, part),
            held(PIECES, ALL, part),
            held(CAP, WIDTH),
            held(CAP, WIDTH),
            held(CAP, WIDTH),
            held(WIDTH, 2 * HIDDEN),
            held(2, HIDDEN, HALF),
            held32(CAP, 2 * HIDDEN),
            held32(CAP, HIDDEN),
            held(CAP, HIDDEN),
            held(HIDDEN, CAP),
            held(CAP, 2 * HIDDEN),
            pltpu.VMEM((16, TOK), jnp.int32),
            held(ALL, CAP),
            held(CAP, ALL),
            held(ALL, CAP),
            held(CAP, ALL),
            held32(CAP, 1),
            held32(CAP, 1),
            held32(CAP, CAP),
            held32(TOK, WIDTH),
            held(3, PIECES, TOK, PIECE),
            held(3, PIECES, TOK, PIECE),
            held(TOK, PIECE),
            held(HALF, 2 * HIDDEN),
            held(HALF, 2 * HIDDEN),
            held(HIDDEN, HALF),
            held(HIDDEN, HALF),
            held32(8, TOK),
            held32(3, 8, TOK),
            held32(8, TOK),
            held32(16 * 8, TOK),
            held(TOK, WIDTH),
            held(TOK, WIDTH),
            dma((4,)),
            dma((4,)),
            dma((PIECES,)),
            dma((PIECES,)),
            dma((3,)),
            dma((3,)),
            dma((3,)),
            dma((4, 4)),
            dma((4, 4)),
            dma((3, PIECES)),
            dma((3, PIECES)),
            dma((2,)),
            dma((2,)),
            dma((2,)),
            dma((3,)),
            dma((3,)),
            dma,
            dma,
            dma((PIECES,)),
            dma((PIECES,)),
        ],
        compiler_params=pltpu.CompilerParams(
            collective_id=0, has_side_effects=True, vmem_limit_bytes=56 * 2**20
        ),
        cost_estimate=pl.CostEstimate(
            flops=8_000_000_000, bytes_accessed=8_000_000, transcendentals=131072
        ),
    )(
        layer_input[0, 0],
        grad_output[0, 0],
        selections[0, 0],
        gate_values[0, 0],
        gate_weight[0, 0],
        up_weight[0, 0],
        down_weight[0, 0],
    )

    def blocks(*dims):
        return pl.BlockSpec(dims, lambda i: (i, 0))

    outs = pl.pallas_call(
        finish,
        grid=(2,),
        out_shape=(
            shape((TOK, WIDTH), BF16),
            shape((16, CAP), F32),
            shape((HALF, HIDDEN), F32),
            shape((HALF, HIDDEN), F32),
            shape((HIDDEN, HALF), F32),
        ),
        in_specs=[
            blocks(TOK // 2, WIDTH),
            blocks(8, CAP),
            blocks(CAP, 2 * HIDDEN),
            blocks(CAP, 2 * HIDDEN),
            blocks(TOK, HALF),
            blocks(TOK, HALF),
        ],
        out_specs=(
            blocks(TOK // 2, WIDTH),
            blocks(8, CAP),
            blocks(CAP, HIDDEN),
            blocks(CAP, HIDDEN),
            blocks(TOK, HALF),
        ),
        compiler_params=pltpu.CompilerParams(vmem_limit_bytes=60 * 2**20),
        cost_estimate=pl.CostEstimate(
            flops=1_000_000, bytes_accessed=7_500_000, transcendentals=0
        ),
    )(*middle)
    return tuple(out[None, None] for out in outs)


def solution(mesh):
    return jax.shard_map(
        on_device,
        mesh=mesh,
        in_specs=(
            P("section", "dp", "expert", None),
            P("section", "dp", "expert", None),
            P("section", "dp", None, None),
            P("section", "dp", None, None),
            P("section", "expert", "dp", None),
            P("section", "expert", "dp", None),
            P("section", "expert", None, "dp"),
        ),
        out_specs=(
            P("section", "dp", "expert", None),
            P("section", "dp", None, None),
            P("section", "expert", "dp", None),
            P("section", "expert", "dp", None),
            P("section", "expert", None, "dp"),
        ),
        check_vma=False,
    )
```

```python
import jax
import jax.numpy as jnp
from jax import lax
from jax.experimental import pallas as pl
from jax.experimental.pallas import tpu as pltpu
from jax.sharding import PartitionSpec as P

MESH = pl.DeviceIdType.MESH
BF16 = jnp.bfloat16
F32 = jnp.float32

TOK = 128
WIDTH = 2048
HIDDEN = 256
RANKS = 64
MSG = 16
ALL = RANKS * MSG
CAP = 512
HALF = 1024
PIECES = 4
PIECE = WIDTH // PIECES
SIDE = PIECE // 2
CHUNKS = ((0, 0, 1024), (0, 1024, 1024), (1, 0, 1024), (1, 1024, 1024))


def dot(left, right):
    return lax.dot_general(left, right, (((1,), (0,)), ((), ())), preferred_element_type=F32)


def dot_last(left, right):
    return lax.dot_general(left, right, (((1,), (1,)), ((), ())), preferred_element_type=F32)


def dot_first(left, right):
    return lax.dot_general(left, right, (((0,), (0,)), ((), ())), preferred_element_type=F32)


def iota(shape, dim):
    return lax.broadcasted_iota(jnp.int32, shape, dim)


def one_if(condition):
    return jnp.where(condition, 1.0, 0.0)


def ones_if(condition):
    return one_if(condition).astype(BF16)


def rows_at(index, size):
    return pl.ds(pl.multiple_of(index * size, size), size)


def flip(rank):
    return rank + 1 - 2 * (rank % 2)


def slot_codes(sel, columns, block):
    tokens = (block * TOK + iota((CAP, TOK), 1)).astype(F32)
    taken = jnp.concatenate(
        [
            jnp.sum(one_if(columns[:, e : e + 1] == tokens), axis=0, keepdims=True)
            for e in range(16)
        ],
        axis=0,
    )
    upper = ones_if(iota((TOK, TOK), 0) < iota((TOK, TOK), 1))
    index = dot(taken.astype(BF16), upper).astype(jnp.int32)
    start = jnp.sum(one_if(sel < block * TOK), axis=1, keepdims=True).astype(jnp.int32)
    return jnp.where(taken > 0.5, ((start + index) & 3) * 16 + (index >> 2), -1)


def slot_selector(mine, member, part):
    row = part * TOK + iota((TOK, CAP), 0)
    bound = (row >> 4) * TOK
    ones = jnp.ones((CAP, TOK), F32).astype(BF16)
    before = dot(ones_if(mine < bound), ones).astype(jnp.int32)
    after = dot(ones_if(mine < bound + TOK), ones).astype(jnp.int32)
    slot = iota((TOK, TOK), 0) & 3
    index = 4 * slot + ((member + 1024 - before) & 3)
    hit = (index < after - before) & (((before + index) >> 2) == iota((TOK, TOK), 1))
    return one_if(hit)


def quarter(shape, dim, which):
    return ((iota(shape, dim) >> 2) & 3) == which


def spread_rows(selector, source, start, width, target):
    part = width // 4

    def step(i, carry):
        stacked = jnp.concatenate(
            [source[:, start + s * part : start + (s + 1) * part] for s in range(4)], axis=0
        )
        target[rows_at(i, 256), :] = dot(selector[rows_at(i, 256), :], stacked).astype(BF16)
        return carry

    lax.fori_loop(0, 4, step, 0)


def kernel(
    rows,
    grads,
    sel,
    gates,
    gate_w,
    up_w,
    down_w,
    incoming,
    gate_grad,
    gu_own,
    gu_other,
    down_own,
    down_other,
    send_wide,
    recv_wide,
    send_back,
    recv_back,
    rows_all,
    grads_all,
    gated_all,
    gu_full,
    down_full,
    pre_all,
    ups_all,
    act_all,
    act_t,
    gg_all,
    codes,
    to_slot,
    from_token,
    place_of,
    place_from,
    gate_col,
    part_col,
    place_mat,
    part_own,
    part_relay,
    first_send,
    first_recv,
    second_send,
    second_recv,
    summed,
    gu_send,
    gu_keep,
    down_send,
    down_keep,
    gsend,
    grecv,
    gsum,
    gall,
    combined,
    arrived,
    s_fwd,
    r_fwd,
    s_back,
    r_back,
    s_w,
    r_w,
    s_own,
    s_gather,
    r_gather,
    s_first,
    r_first,
    s_second,
    r_second,
    s_term,
    r_term,
    s_out,
    s_gate,
    r_gate,
    s_spread,
    r_spread,
    s_fin,
    r_fin,
):
    section = lax.axis_index("section")
    me = lax.axis_index("expert")
    dp = lax.axis_index("dp")
    plane = me // 8
    spot = me % 8
    owner = me // 4
    member = me % 4
    mx = flip(member)
    my = (member + 2) % 4
    md = flip(my)
    near_x = owner * 4 + mx
    near_y = owner * 4 + my
    far = owner * 4 + md
    mirror = flip(me)

    def remote(source, target, s_sem, r_sem, where):
        return pltpu.make_async_remote_copy(
            src_ref=source,
            dst_ref=target,
            send_sem=s_sem,
            recv_sem=r_sem,
            device_id=where,
            device_id_type=MESH,
        )

    def await_copy(view, sem):
        pltpu.make_async_copy(view, view, sem).wait()

    barrier = pltpu.get_barrier_semaphore()

    def greet(i, carry):
        pl.semaphore_signal(
            barrier, inc=1, device_id={"expert": (me + i) % RANKS}, device_id_type=MESH
        )
        return carry

    lax.fori_loop(1, RANKS, greet, 0)
    pl.semaphore_signal(barrier, inc=1, device_id={"dp": 1 - dp}, device_id_type=MESH)
    pl.semaphore_signal(
        barrier, inc=1, device_id={"section": 1 - section, "expert": mirror}, device_id_type=MESH
    )

    gate_cols, up_cols = pl.ds(0, HIDDEN), pl.ds(HIDDEN, HIDDEN)
    weight_views = [
        (gate_w, gu_full.at[rows_at(dp, HALF), gate_cols]),
        (up_w, gu_full.at[rows_at(dp, HALF), up_cols]),
        (down_w, down_full.at[dp]),
    ]
    own_copies = [
        pltpu.make_async_copy(source, target, s_own.at[i])
        for i, (source, target) in enumerate(weight_views)
    ]
    for copy in own_copies:
        copy.start()

    send_fwd = [send_wide.at[i] for i in range(4)]
    recv_fwd = [recv_wide.at[i] for i in range(4)]

    columns = jnp.transpose(sel[...].astype(F32))
    codes[...] = slot_codes(sel[...], columns, me)

    def make_to_slot(e, carry):
        line = iota((64, TOK), 0)
        hit = codes[pl.ds(e, 1), :] == line - (line & 12)
        for s in range(4):
            to_slot[rows_at(e, 64), s * TOK : (s + 1) * TOK] = ones_if(
                hit & quarter((64, TOK), 0, s)
            )
        return carry

    lax.fori_loop(0, 16, make_to_slot, 0)
    def fill(i):
        array, start, width = CHUNKS[i]
        spread_rows(to_slot, (rows, grads)[array], start, width, send_fwd[i])

    fill(0)

    pl.semaphore_wait(barrier, RANKS + 1)

    planes = [((plane + dz) % 8) * 8 for dz in (4, 1, 7, 2, 6, 3, 5, 0)]

    def exchange(source, target, s_sem, r_sem, mirrored):
        def send(to):
            block = flip(to) if mirrored else to
            remote(
                source.at[rows_at(block, MSG)],
                target.at[rows_at(me, MSG)],
                s_sem,
                r_sem,
                {"expert": to},
            ).start()

        def step(i, carry):
            place = (spot + i) % 8
            for start in planes:
                send(start + place)
            return carry

        for start in planes[:-1]:
            send(start + spot)
        lax.fori_loop(1, 8, step, 0)
        block = flip(me) if mirrored else me
        target[rows_at(me, MSG), :] = source[rows_at(block, MSG), :]

    def drain(ref, sem):
        await_copy(ref.at[pl.ds(0, (RANKS - 1) * MSG)], sem)

    def dispatch(i):
        exchange(send_fwd[i], recv_fwd[i], s_fwd.at[i], r_fwd.at[i], False)

    dispatch(0)
    partner = {"dp": 1 - dp}
    weight_copies = [
        remote(source, target, s_w.at[i], r_w.at[i], partner)
        for i, (source, target) in enumerate(weight_views)
    ]
    for copy in weight_copies:
        copy.start()
    for i in range(1, 4):
        fill(i)

    mine = sel[pl.ds(owner, 1), :]

    def make_place(part, carry):
        tile = slot_selector(mine, member, part)
        turned = jnp.transpose(tile)
        for s in range(4):
            keep = slice(s * TOK, (s + 1) * TOK)
            place_of[rows_at(part, TOK), keep] = (
                tile * one_if(quarter((TOK, TOK), 0, s))
            ).astype(BF16)
            place_from[keep, rows_at(part, TOK)] = (
                turned * one_if(quarter((TOK, TOK), 1, s))
            ).astype(BF16)
        return carry

    lax.fori_loop(0, 8, make_place, 0)

    def make_tables():
        across = iota((CAP, CAP), 1)
        down = iota((CAP, CAP), 0)
        mine_f = mine.astype(F32)
        mine_col = jnp.sum(jnp.where(across == down, mine_f, 0.0), axis=1, keepdims=True)
        rank = jnp.sum(one_if(mine_col < mine_f), axis=0, keepdims=True).astype(jnp.int32)
        place = (rank & 3) * TOK + (rank >> 2)
        place_mat[...] = one_if(place == down)
        gate_col[...] = jnp.sum(
            jnp.where(place_mat[...] > 0.5, gates[pl.ds(owner, 1), :], 0.0), axis=1, keepdims=True
        )

    def make_from_token():
        codes[...] = slot_codes(sel[...], columns, mirror)

        def step(pair, carry):
            line = iota((TOK, TOK), 0)
            inner = line & 63
            wanted = jnp.where(
                line < 64, codes[pl.ds(2 * pair, 1), :], codes[pl.ds(2 * pair + 1, 1), :]
            )
            turned = jnp.transpose(one_if(wanted == inner - (inner & 12)))
            for s in range(4):
                from_token[s * TOK : (s + 1) * TOK, rows_at(pair, TOK)] = (
                    turned * one_if(quarter((TOK, TOK), 1, s))
                ).astype(BF16)
            return carry

        lax.fori_loop(0, 8, step, 0)

    def view_of(i, block, offset, width):
        array, start, _ = CHUNKS[i]
        return (rows_all, grads_all)[array].at[rows_at(block, TOK), pl.ds(start + offset, width)]

    def full_view(i, block):
        return view_of(i, block, 0, CHUNKS[i][2])

    def low_view(i, block):
        return view_of(i, block, 0, CHUNKS[i][2] // 2)

    def high_view(i, block):
        return view_of(i, block, CHUNKS[i][2] // 2, CHUNKS[i][2] // 2)

    def gather_copy(i, step, view, to):
        return remote(view, view, s_gather.at[i, step], r_gather.at[i, step], {"expert": to})

    def gather_own(i):
        drain(send_fwd[i], s_fwd.at[i])
        if i < 3:
            dispatch(i + 1)
        drain(recv_fwd[i], r_fwd.at[i])
        compacted = dot(place_from[...], recv_fwd[i][...])
        array, start, width = CHUNKS[i]
        part = width // 4
        for s in range(4):
            (rows_all, grads_all)[array][
                rows_at(member, TOK), start + s * part : start + (s + 1) * part
            ] = compacted[s * TOK : (s + 1) * TOK, :].astype(BF16)
        own = full_view(i, member)
        gather_copy(i, 0, own, near_x).start()
        gather_copy(i, 1, own, near_y).start()

    def gather_forward(i):
        await_copy(full_view(i, mx), r_gather.at[i, 0])
        gather_copy(i, 2, low_view(i, mx), near_y).start()
        await_copy(full_view(i, my), r_gather.at[i, 1])
        gather_copy(i, 3, high_view(i, my), near_x).start()

    def gather_far(i):
        await_copy(low_view(i, md), r_gather.at[i, 2])
        await_copy(high_view(i, md), r_gather.at[i, 3])

    def gather_sent(i):
        await_copy(full_view(i, member), s_gather.at[i, 0])
        await_copy(full_view(i, member), s_gather.at[i, 1])
        await_copy(low_view(i, mx), s_gather.at[i, 2])
        await_copy(high_view(i, my), s_gather.at[i, 3])

    def forward(i, block):
        at = rows_at(block, TOK)
        half = slice(i * HALF, (i + 1) * HALF)
        product = dot(rows_all[at, half], gu_full[half, :])
        pre_all[at, :] = product if i == 0 else pre_all[at, :] + product

    def upstream(i, block):
        at = rows_at(block, TOK)
        _, start, width = CHUNKS[i]
        columns = slice(start, start + width)
        grad = grads_all[at, columns]
        gated_all[at, columns] = (gate_col[at, :] * grad.astype(F32)).astype(BF16)
        inner = start % HALF
        product = dot_last(grad, down_full[start // HALF, :, inner : inner + width])
        ups_all[at, :] = product if start == 0 else ups_all[at, :] + product

    def backward(block):
        at = rows_at(block, TOK)
        ups, pre, up = ups_all[at, :], pre_all[at, :HIDDEN], pre_all[at, HIDDEN:]
        sigmoid = jax.nn.sigmoid(pre)
        swish = pre * sigmoid
        activation = (swish * up).astype(BF16)
        part_col[at, :] = jnp.sum(activation.astype(F32) * ups, axis=1, keepdims=True)
        scaled = gate_col[at, :] * ups
        act_all[at, :] = activation
        gg_all[at, :HIDDEN] = (scaled * up * sigmoid * (1.0 + pre * (1.0 - sigmoid))).astype(BF16)
        gg_all[at, HIDDEN:] = (scaled * swish).astype(BF16)

    def input_part(block, c):
        return dot_last(gg_all[rows_at(block, TOK), :], gu_full[c * PIECE : (c + 1) * PIECE, :])

    def first_copy(axis, c, slot):
        return remote(
            first_send.at[axis, c, slot],
            first_recv.at[axis, c, slot],
            s_first.at[axis, c, slot],
            r_first.at[axis, c, slot],
            {"expert": (near_x, near_y)[axis]},
        )

    def second_copy(axis, c):
        return remote(
            second_send.at[axis, c],
            second_recv.at[axis, c],
            s_second.at[axis, c],
            r_second.at[axis, c],
            {"expert": (near_x, near_y)[axis]},
        )

    def first_near(c):
        for axis, block in enumerate((mx, my)):
            product = input_part(block, c)
            sides = (product[:, :SIDE], product[:, SIDE:])
            first_send[axis, c, 0] = sides[axis].astype(BF16)
            part_relay[axis, c] = sides[1 - axis]
            first_copy(axis, c, 0).start()

    def first_far(c):
        product = input_part(md, c).astype(BF16)
        for axis in range(2):
            first_send[axis, c, 1] = product[:, axis * SIDE : (axis + 1) * SIDE]
            first_copy(axis, c, 1).start()

    def relay(c):
        for axis in range(2):
            other = 1 - axis
            await_copy(first_recv.at[axis, c, 1], r_first.at[axis, c, 1])
            second_send[other, c] = (part_relay[other, c] + first_recv[axis, c, 1].astype(F32)).astype(
                BF16
            )
            second_copy(other, c).start()

    gather_own(0)
    make_tables()
    gather_forward(0)
    for i, (source, target) in enumerate(weight_views):
        await_copy(target, s_own.at[i])
    for i, view in enumerate(
        (
            gu_full.at[rows_at(1 - dp, HALF), gate_cols],
            gu_full.at[rows_at(1 - dp, HALF), up_cols],
            down_full.at[1 - dp],
        )
    ):
        await_copy(view, r_w.at[i])
    gather_own(1)
    for block in (member, mx, my):
        forward(0, block)
    make_from_token()
    gather_far(0)
    gather_forward(1)
    gather_own(2)
    forward(0, md)
    for block in (member, mx, my):
        forward(1, block)
    upstream(2, member)
    gather_far(1)
    gather_forward(2)
    gather_own(3)
    forward(1, md)
    upstream(2, mx)
    upstream(2, my)
    upstream(3, member)
    backward(member)
    for c in range(PIECES):
        part_own[:, c * PIECE : (c + 1) * PIECE] = input_part(member, c)
    gather_far(2)
    upstream(2, md)
    gather_forward(3)
    for block in (mx, my):
        upstream(3, block)
        backward(block)
    first_near(0)
    gather_far(3)
    upstream(3, md)
    backward(md)
    first_far(0)

    for b in range(4):
        act_t[:, b * TOK : (b + 1) * TOK] = jnp.transpose(
            act_all[b * TOK : (b + 1) * TOK, :].astype(F32)
        ).astype(BF16)

    def weight_terms(half, gu_to, down_to):
        def step(i, carry):
            columns = pl.ds(pl.multiple_of(half * HALF + i * 256, 256), 256)
            gu_to[rows_at(i, 256), :] = dot_first(rows_all[:, columns], gg_all[...]).astype(BF16)
            down_to[:, rows_at(i, 256)] = dot(act_t[...], gated_all[:, columns]).astype(BF16)
            return carry

        lax.fori_loop(0, 4, step, 0)

    first_far(1)
    first_near(1)
    weight_terms(1 - dp, gu_send, down_send)
    term_copies = [
        remote(gu_send, gu_other, s_term.at[0], r_term.at[0], partner),
        remote(down_send, down_other, s_term.at[1], r_term.at[1], partner),
    ]
    for copy in term_copies:
        copy.start()

    def give_back(c):
        for axis in range(2):
            await_copy(first_recv.at[axis, c, 0], r_first.at[axis, c, 0])
            await_copy(second_recv.at[1 - axis, c], r_second.at[1 - axis, c])
            start = c * PIECE + axis * SIDE
            summed[:, axis * SIDE : (axis + 1) * SIDE] = (
                part_own[:, start : start + SIDE]
                + first_recv[axis, c, 0].astype(F32)
                + second_recv[1 - axis, c].astype(F32)
            ).astype(BF16)
        spread_rows(place_of, summed, 0, PIECE, send_back.at[c])
        exchange(send_back.at[c], recv_back.at[c], s_back.at[c], r_back.at[c], True)

    def last_copy(c):
        view = pl.ds(c * PIECE, PIECE)
        return remote(
            combined.at[:, view],
            arrived.at[:, view],
            s_fin.at[c],
            r_fin.at[c],
            {"section": 0, "expert": mirror},
        )

    def combine(c):
        drain(recv_back.at[c], r_back.at[c])
        sums = dot(from_token[...], recv_back[c]).astype(BF16)
        part = PIECE // 4
        for s in range(4):
            start = c * PIECE + s * part
            combined[:, start : start + part] = sums[s * TOK : (s + 1) * TOK, :]

        @pl.when(section == 1)
        def _():
            last_copy(c).start()

    relay(0)
    first_far(2)
    first_near(2)
    give_back(0)
    relay(1)
    first_far(3)
    first_near(3)

    part_row = jnp.sum(place_mat[...] * part_col[...], axis=0, keepdims=True)
    gsend[...] = jnp.zeros((8, TOK), F32)
    for i in range(4):
        gsend[i : i + 1, :] = part_row[:, i * TOK : (i + 1) * TOK]
    gate_copies = [
        remote(gsend, grecv.at[i], s_gate.at[i], r_gate.at[i], {"expert": to})
        for i, to in enumerate((near_x, near_y, far))
    ]
    for copy in gate_copies:
        copy.start()

    give_back(1)
    relay(2)

    for copy in gate_copies:
        copy.wait_recv()
    gsum[...] = (gsend[...] + grecv[0]) + (grecv[1] + grecv[2])

    def spread_gate(i, carry):
        to = ((owner + i) % 16) * 4 + member
        remote(gsum, gall.at[rows_at(owner, 8)], s_spread, r_spread, {"expert": to}).start()
        return carry

    lax.fori_loop(1, 16, spread_gate, 0)
    gall[rows_at(owner, 8), :] = gsum[...]

    give_back(2)
    relay(3)
    combine(0)
    give_back(3)
    weight_terms(dp, gu_keep, down_keep)
    out_copies = [
        pltpu.make_async_copy(gu_keep, gu_own, s_out.at[0]),
        pltpu.make_async_copy(down_keep, down_own, s_out.at[1]),
    ]
    for copy in out_copies:
        copy.start()
    combine(1)
    combine(2)

    others = gall.at[pl.ds(0, 15 * 8)]
    await_copy(others, r_spread)
    for e in range(16):
        for i in range(4):
            gate_grad[e : e + 1, i * TOK : (i + 1) * TOK] = gall[e * 8 + i : e * 8 + i + 1, :]

    combine(3)

    for i in range(4):
        gather_sent(i)
    for c in range(PIECES):
        drain(send_back.at[c], s_back.at[c])
        for axis in range(2):
            for slot in range(2):
                await_copy(first_send.at[axis, c, slot], s_first.at[axis, c, slot])
            await_copy(second_send.at[axis, c], s_second.at[axis, c])
    for copy in (*weight_copies, *gate_copies, *term_copies):
        copy.wait_send()
    await_copy(others, s_spread)
    for copy in term_copies:
        copy.wait_recv()
    for copy in out_copies:
        copy.wait()

    @pl.when(section == 1)
    def _():
        incoming[...] = jnp.zeros((TOK, WIDTH), BF16)
        for c in range(PIECES):
            last_copy(c).wait_send()

    @pl.when(section == 0)
    def _():
        for c in range(PIECES):
            last_copy(c).wait_recv()
            keep = slice(c * PIECE, (c + 1) * PIECE)
            incoming[:, keep] = arrived[:, keep]


def finish(
    incoming, gate_grad, gu_own, gu_other, down_own, down_other, *outs
):
    incoming_to, gate_grad_to, gate_to, up_to, down_to = outs
    incoming_to[...] = incoming[...]
    gate_grad_to[...] = gate_grad[...]
    total = (gu_own[...].astype(F32) + gu_other[...].astype(F32)) * 0.5
    gate_to[...] = total[:, :HIDDEN]
    up_to[...] = total[:, HIDDEN:]
    down_to[...] = (down_own[...].astype(F32) + down_other[...].astype(F32)) * 0.5


def on_device(
    layer_input, grad_output, selections, gate_values, gate_weight, up_weight, down_weight
):
    vmem = pl.BlockSpec(memory_space=pltpu.VMEM)
    hbm = pl.BlockSpec(memory_space=pl.ANY)
    shape = jax.ShapeDtypeStruct
    dma = pltpu.SemaphoreType.DMA

    def held(*dims):
        return pltpu.VMEM(dims, BF16)

    def held32(*dims):
        return pltpu.VMEM(dims, F32)

    part = PIECE // 4
    middle = pl.pallas_call(
        kernel,
        out_shape=(
            shape((TOK, WIDTH), BF16),
            shape((16, CAP), F32),
            shape((HALF, 2 * HIDDEN), BF16),
            shape((HALF, 2 * HIDDEN), BF16),
            shape((HIDDEN, HALF), BF16),
            shape((HIDDEN, HALF), BF16),
        ),
        in_specs=[vmem] * 4 + [hbm] * 3,
        out_specs=(vmem, vmem, hbm, hbm, hbm, hbm),
        scratch_shapes=[
            held(4, ALL, 256),
            held(4, ALL, 256),
            held(PIECES, ALL, part),
            held(PIECES, ALL, part),
            held(CAP, WIDTH),
            held(CAP, WIDTH),
            held(CAP, WIDTH),
            held(WIDTH, 2 * HIDDEN),
            held(2, HIDDEN, HALF),
            held32(CAP, 2 * HIDDEN),
            held32(CAP, HIDDEN),
            held(CAP, HIDDEN),
            held(HIDDEN, CAP),
            held(CAP, 2 * HIDDEN),
            pltpu.VMEM((16, TOK), jnp.int32),
            held(ALL, CAP),
            held(CAP, ALL),
            held(ALL, CAP),
            held(CAP, ALL),
            held32(CAP, 1),
            held32(CAP, 1),
            held32(CAP, CAP),
            held32(TOK, WIDTH),
            held32(2, PIECES, TOK, SIDE),
            held(2, PIECES, 2, TOK, SIDE),
            held(2, PIECES, 2, TOK, SIDE),
            held(2, PIECES, TOK, SIDE),
            held(2, PIECES, TOK, SIDE),
            held(TOK, PIECE),
            held(HALF, 2 * HIDDEN),
            held(HALF, 2 * HIDDEN),
            held(HIDDEN, HALF),
            held(HIDDEN, HALF),
            held32(8, TOK),
            held32(3, 8, TOK),
            held32(8, TOK),
            held32(16 * 8, TOK),
            held(TOK, WIDTH),
            held(TOK, WIDTH),
            dma((4,)),
            dma((4,)),
            dma((PIECES,)),
            dma((PIECES,)),
            dma((3,)),
            dma((3,)),
            dma((3,)),
            dma((4, 4)),
            dma((4, 4)),
            dma((2, PIECES, 2)),
            dma((2, PIECES, 2)),
            dma((2, PIECES)),
            dma((2, PIECES)),
            dma((2,)),
            dma((2,)),
            dma((2,)),
            dma((3,)),
            dma((3,)),
            dma,
            dma,
            dma((PIECES,)),
            dma((PIECES,)),
        ],
        compiler_params=pltpu.CompilerParams(
            collective_id=0, has_side_effects=True, vmem_limit_bytes=56 * 2**20
        ),
        cost_estimate=pl.CostEstimate(
            flops=8_000_000_000, bytes_accessed=8_000_000, transcendentals=131072
        ),
    )(
        layer_input[0, 0],
        grad_output[0, 0],
        selections[0, 0],
        gate_values[0, 0],
        gate_weight[0, 0],
        up_weight[0, 0],
        down_weight[0, 0],
    )

    def blocks(*dims):
        return pl.BlockSpec(dims, lambda i: (i, 0))

    fixed = pl.BlockSpec((16, CAP), lambda i: (0, 0))

    outs = pl.pallas_call(
        finish,
        grid=(2,),
        out_shape=(
            shape((TOK, WIDTH), BF16),
            shape((16, CAP), F32),
            shape((HALF, HIDDEN), F32),
            shape((HALF, HIDDEN), F32),
            shape((HIDDEN, HALF), F32),
        ),
        in_specs=[
            blocks(TOK // 2, WIDTH),
            fixed,
            blocks(HALF // 2, 2 * HIDDEN),
            blocks(HALF // 2, 2 * HIDDEN),
            blocks(HIDDEN // 2, HALF),
            blocks(HIDDEN // 2, HALF),
        ],
        out_specs=(
            blocks(TOK // 2, WIDTH),
            fixed,
            blocks(HALF // 2, HIDDEN),
            blocks(HALF // 2, HIDDEN),
            blocks(HIDDEN // 2, HALF),
        ),
        compiler_params=pltpu.CompilerParams(vmem_limit_bytes=60 * 2**20),
        cost_estimate=pl.CostEstimate(
            flops=1_000_000, bytes_accessed=7_500_000, transcendentals=0
        ),
    )(*middle)
    return tuple(out[None, None] for out in outs)


def solution(mesh):
    return jax.shard_map(
        on_device,
        mesh=mesh,
        in_specs=(
            P("section", "dp", "expert", None),
            P("section", "dp", "expert", None),
            P("section", "dp", None, None),
            P("section", "dp", None, None),
            P("section", "expert", "dp", None),
            P("section", "expert", "dp", None),
            P("section", "expert", None, "dp"),
        ),
        out_specs=(
            P("section", "dp", "expert", None),
            P("section", "dp", None, None),
            P("section", "expert", "dp", None),
            P("section", "expert", "dp", None),
            P("section", "expert", None, "dp"),
        ),
        check_vma=False,
    )
```

```python
import jax
import jax.numpy as jnp
from jax import lax
from jax.experimental import pallas as pl
from jax.experimental.pallas import tpu as pltpu
from jax.sharding import PartitionSpec as P

MESH = pl.DeviceIdType.MESH
BF16 = jnp.bfloat16
F32 = jnp.float32

TOK = 128
WIDTH = 2048
HIDDEN = 256
RANKS = 64
MSG = 16
ALL = RANKS * MSG
CAP = 512
HALF = 1024
PIECES = 4
PIECE = WIDTH // PIECES
SIDE = PIECE // 2
CHUNKS = ((0, 0, 1024), (0, 1024, 1024), (1, 0, 1024), (1, 1024, 1024))


def dot(left, right):
    return lax.dot_general(left, right, (((1,), (0,)), ((), ())), preferred_element_type=F32)


def dot_last(left, right):
    return lax.dot_general(left, right, (((1,), (1,)), ((), ())), preferred_element_type=F32)


def dot_first(left, right):
    return lax.dot_general(left, right, (((0,), (0,)), ((), ())), preferred_element_type=F32)


def iota(shape, dim):
    return lax.broadcasted_iota(jnp.int32, shape, dim)


def one_if(condition):
    return jnp.where(condition, 1.0, 0.0)


def ones_if(condition):
    return one_if(condition).astype(BF16)


def rows_at(index, size):
    return pl.ds(pl.multiple_of(index * size, size), size)


def flip(rank):
    return rank + 1 - 2 * (rank % 2)


def slot_codes(sel, columns, block):
    tokens = (block * TOK + iota((CAP, TOK), 1)).astype(F32)
    taken = jnp.concatenate(
        [
            jnp.sum(one_if(columns[:, e : e + 1] == tokens), axis=0, keepdims=True)
            for e in range(16)
        ],
        axis=0,
    )
    upper = ones_if(iota((TOK, TOK), 0) < iota((TOK, TOK), 1))
    index = dot(taken.astype(BF16), upper).astype(jnp.int32)
    start = jnp.sum(one_if(sel < block * TOK), axis=1, keepdims=True).astype(jnp.int32)
    return jnp.where(taken > 0.5, ((start + index) & 3) * 16 + (index >> 2), -1)


def slot_selector(mine, member, part):
    row = part * TOK + iota((TOK, CAP), 0)
    bound = (row >> 4) * TOK
    ones = jnp.ones((CAP, TOK), F32).astype(BF16)
    before = dot(ones_if(mine < bound), ones).astype(jnp.int32)
    after = dot(ones_if(mine < bound + TOK), ones).astype(jnp.int32)
    slot = iota((TOK, TOK), 0) & 3
    index = 4 * slot + ((member + 1024 - before) & 3)
    hit = (index < after - before) & (((before + index) >> 2) == iota((TOK, TOK), 1))
    return one_if(hit)


def quarter(shape, dim, which):
    return ((iota(shape, dim) >> 2) & 3) == which


def spread_rows(selector, source, start, width, target):
    part = width // 4

    def step(i, carry):
        stacked = jnp.concatenate(
            [source[:, start + s * part : start + (s + 1) * part] for s in range(4)], axis=0
        )
        target[rows_at(i, 256), :] = dot(selector[rows_at(i, 256), :], stacked).astype(BF16)
        return carry

    lax.fori_loop(0, 4, step, 0)


def kernel(
    rows_from,
    grads_from,
    sel,
    gates,
    gate_w,
    up_w,
    down_w,
    incoming,
    gate_grad,
    gu_own,
    gu_other,
    down_own,
    down_other,
    rows,
    grads,
    send_wide,
    recv_wide,
    send_back,
    recv_back,
    rows_all,
    grads_all,
    gated_all,
    gu_full,
    down_full,
    pre_all,
    ups_all,
    act_all,
    act_t,
    gg_all,
    codes,
    to_slot,
    from_token,
    place_of,
    place_from,
    gate_col,
    part_col,
    place_mat,
    part_own,
    part_relay,
    first_send,
    first_recv,
    second_send,
    second_recv,
    summed,
    gu_send,
    gu_keep,
    down_send,
    down_keep,
    gsend,
    grecv,
    gsum,
    gall,
    combined,
    zeros,
    s_load,
    s_fwd,
    r_fwd,
    s_back,
    r_back,
    s_w,
    r_w,
    s_own,
    s_gather,
    r_gather,
    s_first,
    r_first,
    s_second,
    r_second,
    s_term,
    r_term,
    s_out,
    s_gate,
    r_gate,
    s_spread,
    r_spread,
    s_fin,
    r_fin,
):
    section = lax.axis_index("section")
    me = lax.axis_index("expert")
    dp = lax.axis_index("dp")
    plane = me // 8
    spot = me % 8
    owner = me // 4
    member = me % 4
    mx = flip(member)
    my = (member + 2) % 4
    md = flip(my)
    near_x = owner * 4 + mx
    near_y = owner * 4 + my
    far = owner * 4 + md
    mirror = flip(me)

    def remote(source, target, s_sem, r_sem, where):
        return pltpu.make_async_remote_copy(
            src_ref=source,
            dst_ref=target,
            send_sem=s_sem,
            recv_sem=r_sem,
            device_id=where,
            device_id_type=MESH,
        )

    def await_copy(view, sem):
        pltpu.make_async_copy(view, view, sem).wait()

    loads = [
        pltpu.make_async_copy(rows_from, rows, s_load.at[0]),
        pltpu.make_async_copy(grads_from, grads, s_load.at[1]),
    ]
    for copy in loads:
        copy.start()

    barrier = pltpu.get_barrier_semaphore()

    def greet(i, carry):
        pl.semaphore_signal(
            barrier, inc=1, device_id={"expert": (me + i) % RANKS}, device_id_type=MESH
        )
        return carry

    lax.fori_loop(1, RANKS, greet, 0)
    pl.semaphore_signal(barrier, inc=1, device_id={"dp": 1 - dp}, device_id_type=MESH)
    pl.semaphore_signal(
        barrier, inc=1, device_id={"section": 1 - section, "expert": mirror}, device_id_type=MESH
    )

    gate_cols, up_cols = pl.ds(0, HIDDEN), pl.ds(HIDDEN, HIDDEN)
    weight_views = [
        (gate_w, gu_full.at[rows_at(dp, HALF), gate_cols]),
        (up_w, gu_full.at[rows_at(dp, HALF), up_cols]),
        (down_w, down_full.at[dp]),
    ]
    own_copies = [
        pltpu.make_async_copy(source, target, s_own.at[i])
        for i, (source, target) in enumerate(weight_views)
    ]
    for copy in own_copies:
        copy.start()

    send_fwd = [send_wide.at[i] for i in range(4)]
    recv_fwd = [recv_wide.at[i] for i in range(4)]

    columns = jnp.transpose(sel[...].astype(F32))
    codes[...] = slot_codes(sel[...], columns, me)

    def make_to_slot(e, carry):
        line = iota((64, TOK), 0)
        hit = codes[pl.ds(e, 1), :] == line - (line & 12)
        for s in range(4):
            to_slot[rows_at(e, 64), s * TOK : (s + 1) * TOK] = ones_if(
                hit & quarter((64, TOK), 0, s)
            )
        return carry

    lax.fori_loop(0, 16, make_to_slot, 0)
    def fill(i):
        array, start, width = CHUNKS[i]
        spread_rows(to_slot, (rows, grads)[array], start, width, send_fwd[i])

    for copy in loads:
        copy.wait()
    fill(0)

    pl.semaphore_wait(barrier, RANKS + 1)

    planes = [((plane + dz) % 8) * 8 for dz in (4, 1, 7, 2, 6, 3, 5, 0)]

    def exchange(source, target, s_sem, r_sem, mirrored):
        def send(to):
            block = flip(to) if mirrored else to
            remote(
                source.at[rows_at(block, MSG)],
                target.at[rows_at(me, MSG)],
                s_sem,
                r_sem,
                {"expert": to},
            ).start()

        def step(i, carry):
            place = (spot + i) % 8
            for start in planes:
                send(start + place)
            return carry

        for start in planes[:-1]:
            send(start + spot)
        lax.fori_loop(1, 8, step, 0)
        block = flip(me) if mirrored else me
        target[rows_at(me, MSG), :] = source[rows_at(block, MSG), :]

    def drain(ref, sem):
        await_copy(ref.at[pl.ds(0, (RANKS - 1) * MSG)], sem)

    def dispatch(i):
        exchange(send_fwd[i], recv_fwd[i], s_fwd.at[i], r_fwd.at[i], False)

    dispatch(0)
    partner = {"dp": 1 - dp}
    weight_copies = [
        remote(source, target, s_w.at[i], r_w.at[i], partner)
        for i, (source, target) in enumerate(weight_views)
    ]
    for copy in weight_copies:
        copy.start()
    for i in range(1, 4):
        fill(i)

    mine = sel[pl.ds(owner, 1), :]

    def make_place(part, carry):
        tile = slot_selector(mine, member, part)
        turned = jnp.transpose(tile)
        for s in range(4):
            keep = slice(s * TOK, (s + 1) * TOK)
            place_of[rows_at(part, TOK), keep] = (
                tile * one_if(quarter((TOK, TOK), 0, s))
            ).astype(BF16)
            place_from[keep, rows_at(part, TOK)] = (
                turned * one_if(quarter((TOK, TOK), 1, s))
            ).astype(BF16)
        return carry

    lax.fori_loop(0, 8, make_place, 0)

    def make_tables():
        across = iota((CAP, CAP), 1)
        down = iota((CAP, CAP), 0)
        mine_f = mine.astype(F32)
        mine_col = jnp.sum(jnp.where(across == down, mine_f, 0.0), axis=1, keepdims=True)
        rank = jnp.sum(one_if(mine_col < mine_f), axis=0, keepdims=True).astype(jnp.int32)
        place = (rank & 3) * TOK + (rank >> 2)
        place_mat[...] = one_if(place == down)
        gate_col[...] = jnp.sum(
            jnp.where(place_mat[...] > 0.5, gates[pl.ds(owner, 1), :], 0.0), axis=1, keepdims=True
        )

    def make_from_token():
        codes[...] = slot_codes(sel[...], columns, mirror)

        def step(pair, carry):
            line = iota((TOK, TOK), 0)
            inner = line & 63
            wanted = jnp.where(
                line < 64, codes[pl.ds(2 * pair, 1), :], codes[pl.ds(2 * pair + 1, 1), :]
            )
            turned = jnp.transpose(one_if(wanted == inner - (inner & 12)))
            for s in range(4):
                from_token[s * TOK : (s + 1) * TOK, rows_at(pair, TOK)] = (
                    turned * one_if(quarter((TOK, TOK), 1, s))
                ).astype(BF16)
            return carry

        lax.fori_loop(0, 8, step, 0)

    def view_of(i, block, offset, width):
        array, start, _ = CHUNKS[i]
        return (rows_all, grads_all)[array].at[rows_at(block, TOK), pl.ds(start + offset, width)]

    def full_view(i, block):
        return view_of(i, block, 0, CHUNKS[i][2])

    def low_view(i, block):
        return view_of(i, block, 0, CHUNKS[i][2] // 2)

    def high_view(i, block):
        return view_of(i, block, CHUNKS[i][2] // 2, CHUNKS[i][2] // 2)

    def gather_copy(i, step, view, to):
        return remote(view, view, s_gather.at[i, step], r_gather.at[i, step], {"expert": to})

    def gather_own(i):
        drain(send_fwd[i], s_fwd.at[i])
        if i < 3:
            dispatch(i + 1)
        drain(recv_fwd[i], r_fwd.at[i])
        compacted = dot(place_from[...], recv_fwd[i][...])
        array, start, width = CHUNKS[i]
        part = width // 4
        for s in range(4):
            (rows_all, grads_all)[array][
                rows_at(member, TOK), start + s * part : start + (s + 1) * part
            ] = compacted[s * TOK : (s + 1) * TOK, :].astype(BF16)
        own = full_view(i, member)
        gather_copy(i, 0, own, near_x).start()
        gather_copy(i, 1, own, near_y).start()

    def gather_forward(i):
        await_copy(full_view(i, mx), r_gather.at[i, 0])
        gather_copy(i, 2, low_view(i, mx), near_y).start()
        await_copy(full_view(i, my), r_gather.at[i, 1])
        gather_copy(i, 3, high_view(i, my), near_x).start()

    def gather_far(i):
        await_copy(low_view(i, md), r_gather.at[i, 2])
        await_copy(high_view(i, md), r_gather.at[i, 3])

    def gather_sent(i):
        await_copy(full_view(i, member), s_gather.at[i, 0])
        await_copy(full_view(i, member), s_gather.at[i, 1])
        await_copy(low_view(i, mx), s_gather.at[i, 2])
        await_copy(high_view(i, my), s_gather.at[i, 3])

    def forward(i, block):
        at = rows_at(block, TOK)
        half = slice(i * HALF, (i + 1) * HALF)
        product = dot(rows_all[at, half], gu_full[half, :])
        pre_all[at, :] = product if i == 0 else pre_all[at, :] + product

    def upstream(i, block):
        at = rows_at(block, TOK)
        _, start, width = CHUNKS[i]
        columns = slice(start, start + width)
        grad = grads_all[at, columns]
        gated_all[at, columns] = (gate_col[at, :] * grad.astype(F32)).astype(BF16)
        inner = start % HALF
        product = dot_last(grad, down_full[start // HALF, :, inner : inner + width])
        ups_all[at, :] = product if start == 0 else ups_all[at, :] + product

    def backward(block):
        at = rows_at(block, TOK)
        ups, pre, up = ups_all[at, :], pre_all[at, :HIDDEN], pre_all[at, HIDDEN:]
        sigmoid = jax.nn.sigmoid(pre)
        swish = pre * sigmoid
        activation = (swish * up).astype(BF16)
        part_col[at, :] = jnp.sum(activation.astype(F32) * ups, axis=1, keepdims=True)
        scaled = gate_col[at, :] * ups
        act_all[at, :] = activation
        gg_all[at, :HIDDEN] = (scaled * up * sigmoid * (1.0 + pre * (1.0 - sigmoid))).astype(BF16)
        gg_all[at, HIDDEN:] = (scaled * swish).astype(BF16)

    def input_part(block, c):
        return dot_last(gg_all[rows_at(block, TOK), :], gu_full[c * PIECE : (c + 1) * PIECE, :])

    def first_copy(axis, c, slot):
        return remote(
            first_send.at[axis, c, slot],
            first_recv.at[axis, c, slot],
            s_first.at[axis, c, slot],
            r_first.at[axis, c, slot],
            {"expert": (near_x, near_y)[axis]},
        )

    def second_copy(axis, c):
        return remote(
            second_send.at[axis, c],
            second_recv.at[axis, c],
            s_second.at[axis, c],
            r_second.at[axis, c],
            {"expert": (near_x, near_y)[axis]},
        )

    def first_near(c):
        for axis, block in enumerate((mx, my)):
            product = input_part(block, c)
            sides = (product[:, :SIDE], product[:, SIDE:])
            first_send[axis, c, 0] = sides[axis].astype(BF16)
            part_relay[axis, c] = sides[1 - axis]
            first_copy(axis, c, 0).start()

    def first_far(c):
        product = input_part(md, c).astype(BF16)
        for axis in range(2):
            first_send[axis, c, 1] = product[:, axis * SIDE : (axis + 1) * SIDE]
            first_copy(axis, c, 1).start()

    def relay(c):
        for axis in range(2):
            other = 1 - axis
            await_copy(first_recv.at[axis, c, 1], r_first.at[axis, c, 1])
            second_send[other, c] = (part_relay[other, c] + first_recv[axis, c, 1].astype(F32)).astype(
                BF16
            )
            second_copy(other, c).start()

    zeros[...] = jnp.zeros((TOK, WIDTH), BF16)
    blank = pltpu.make_async_copy(zeros, incoming, s_load.at[2])

    @pl.when(section == 1)
    def _():
        blank.start()

    gather_own(0)
    make_tables()
    gather_forward(0)
    for i, (source, target) in enumerate(weight_views):
        await_copy(target, s_own.at[i])
    for i, view in enumerate(
        (
            gu_full.at[rows_at(1 - dp, HALF), gate_cols],
            gu_full.at[rows_at(1 - dp, HALF), up_cols],
            down_full.at[1 - dp],
        )
    ):
        await_copy(view, r_w.at[i])
    gather_own(1)
    for block in (member, mx, my):
        forward(0, block)
    make_from_token()
    gather_far(0)
    gather_forward(1)
    gather_own(2)
    forward(0, md)
    for block in (member, mx, my):
        forward(1, block)
    upstream(2, member)
    gather_far(1)
    gather_forward(2)
    gather_own(3)
    forward(1, md)
    upstream(2, mx)
    upstream(2, my)
    upstream(3, member)
    backward(member)
    for c in range(PIECES):
        part_own[:, c * PIECE : (c + 1) * PIECE] = input_part(member, c)
    gather_far(2)
    upstream(2, md)
    gather_forward(3)
    for block in (mx, my):
        upstream(3, block)
        backward(block)
    first_near(0)
    gather_far(3)
    upstream(3, md)
    backward(md)
    first_far(0)

    for b in range(4):
        act_t[:, b * TOK : (b + 1) * TOK] = jnp.transpose(
            act_all[b * TOK : (b + 1) * TOK, :].astype(F32)
        ).astype(BF16)

    def weight_terms(half, gu_to, down_to):
        def step(i, carry):
            columns = pl.ds(pl.multiple_of(half * HALF + i * 256, 256), 256)
            gu_to[rows_at(i, 256), :] = dot_first(rows_all[:, columns], gg_all[...]).astype(BF16)
            down_to[:, rows_at(i, 256)] = dot(act_t[...], gated_all[:, columns]).astype(BF16)
            return carry

        lax.fori_loop(0, 4, step, 0)

    first_far(1)
    first_near(1)
    weight_terms(1 - dp, gu_send, down_send)
    term_copies = [
        remote(gu_send, gu_other, s_term.at[0], r_term.at[0], partner),
        remote(down_send, down_other, s_term.at[1], r_term.at[1], partner),
    ]
    for copy in term_copies:
        copy.start()

    def give_back(c):
        for axis in range(2):
            await_copy(first_recv.at[axis, c, 0], r_first.at[axis, c, 0])
            await_copy(second_recv.at[1 - axis, c], r_second.at[1 - axis, c])
            start = c * PIECE + axis * SIDE
            summed[:, axis * SIDE : (axis + 1) * SIDE] = (
                part_own[:, start : start + SIDE]
                + first_recv[axis, c, 0].astype(F32)
                + second_recv[1 - axis, c].astype(F32)
            ).astype(BF16)
        spread_rows(place_of, summed, 0, PIECE, send_back.at[c])
        exchange(send_back.at[c], recv_back.at[c], s_back.at[c], r_back.at[c], True)

    def last_copy(c):
        view = pl.ds(c * PIECE, PIECE)
        return remote(
            combined.at[:, view],
            incoming.at[:, view],
            s_fin.at[c],
            r_fin.at[c],
            {"section": 0, "expert": mirror},
        )

    def combine(c):
        drain(recv_back.at[c], r_back.at[c])
        sums = dot(from_token[...], recv_back[c]).astype(BF16)
        part = PIECE // 4
        for s in range(4):
            start = c * PIECE + s * part
            combined[:, start : start + part] = sums[s * TOK : (s + 1) * TOK, :]

        @pl.when(section == 1)
        def _():
            last_copy(c).start()

    relay(0)
    first_far(2)
    first_near(2)
    give_back(0)
    relay(1)
    first_far(3)
    first_near(3)

    part_row = jnp.sum(place_mat[...] * part_col[...], axis=0, keepdims=True)
    gsend[...] = jnp.zeros((8, TOK), F32)
    for i in range(4):
        gsend[i : i + 1, :] = part_row[:, i * TOK : (i + 1) * TOK]
    gate_copies = [
        remote(gsend, grecv.at[i], s_gate.at[i], r_gate.at[i], {"expert": to})
        for i, to in enumerate((near_x, near_y, far))
    ]
    for copy in gate_copies:
        copy.start()

    give_back(1)
    relay(2)

    for copy in gate_copies:
        copy.wait_recv()
    gsum[...] = (gsend[...] + grecv[0]) + (grecv[1] + grecv[2])

    def spread_gate(i, carry):
        to = ((owner + i) % 16) * 4 + member
        remote(gsum, gall.at[rows_at(owner, 8)], s_spread, r_spread, {"expert": to}).start()
        return carry

    lax.fori_loop(1, 16, spread_gate, 0)
    gall[rows_at(owner, 8), :] = gsum[...]

    give_back(2)
    relay(3)
    combine(0)
    give_back(3)
    weight_terms(dp, gu_keep, down_keep)
    out_copies = [
        pltpu.make_async_copy(gu_keep, gu_own, s_out.at[0]),
        pltpu.make_async_copy(down_keep, down_own, s_out.at[1]),
    ]
    for copy in out_copies:
        copy.start()
    combine(1)
    combine(2)

    others = gall.at[pl.ds(0, 15 * 8)]
    await_copy(others, r_spread)
    for e in range(16):
        for i in range(4):
            gate_grad[e : e + 1, i * TOK : (i + 1) * TOK] = gall[e * 8 + i : e * 8 + i + 1, :]

    combine(3)

    for i in range(4):
        gather_sent(i)
    for c in range(PIECES):
        drain(send_back.at[c], s_back.at[c])
        for axis in range(2):
            for slot in range(2):
                await_copy(first_send.at[axis, c, slot], s_first.at[axis, c, slot])
            await_copy(second_send.at[axis, c], s_second.at[axis, c])
    for copy in (*weight_copies, *gate_copies, *term_copies):
        copy.wait_send()
    await_copy(others, s_spread)
    for copy in term_copies:
        copy.wait_recv()
    for copy in out_copies:
        copy.wait()

    @pl.when(section == 1)
    def _():
        for c in range(PIECES):
            last_copy(c).wait_send()
        blank.wait()

    @pl.when(section == 0)
    def _():
        for c in range(PIECES):
            last_copy(c).wait_recv()


def finish(
    incoming, gate_grad, gu_own, gu_other, down_own, down_other, *outs
):
    incoming_to, gate_grad_to, gate_to, up_to, down_to = outs
    incoming_to[...] = incoming[...]
    gate_grad_to[...] = gate_grad[...]
    total = (gu_own[...].astype(F32) + gu_other[...].astype(F32)) * 0.5
    gate_to[...] = total[:, :HIDDEN]
    up_to[...] = total[:, HIDDEN:]
    down_to[...] = (down_own[...].astype(F32) + down_other[...].astype(F32)) * 0.5


def on_device(
    layer_input, grad_output, selections, gate_values, gate_weight, up_weight, down_weight
):
    vmem = pl.BlockSpec(memory_space=pltpu.VMEM)
    hbm = pl.BlockSpec(memory_space=pl.ANY)
    shape = jax.ShapeDtypeStruct
    dma = pltpu.SemaphoreType.DMA

    def held(*dims):
        return pltpu.VMEM(dims, BF16)

    def held32(*dims):
        return pltpu.VMEM(dims, F32)

    part = PIECE // 4
    middle = pl.pallas_call(
        kernel,
        out_shape=(
            shape((TOK, WIDTH), BF16),
            shape((16, CAP), F32),
            shape((HALF, 2 * HIDDEN), BF16),
            shape((HALF, 2 * HIDDEN), BF16),
            shape((HIDDEN, HALF), BF16),
            shape((HIDDEN, HALF), BF16),
        ),
        in_specs=[hbm] * 2 + [vmem] * 2 + [hbm] * 3,
        out_specs=(hbm, vmem, hbm, hbm, hbm, hbm),
        scratch_shapes=[
            held(TOK, WIDTH),
            held(TOK, WIDTH),
            held(4, ALL, 256),
            held(4, ALL, 256),
            held(PIECES, ALL, part),
            held(PIECES, ALL, part),
            held(CAP, WIDTH),
            held(CAP, WIDTH),
            held(CAP, WIDTH),
            held(WIDTH, 2 * HIDDEN),
            held(2, HIDDEN, HALF),
            held32(CAP, 2 * HIDDEN),
            held32(CAP, HIDDEN),
            held(CAP, HIDDEN),
            held(HIDDEN, CAP),
            held(CAP, 2 * HIDDEN),
            pltpu.VMEM((16, TOK), jnp.int32),
            held(ALL, CAP),
            held(CAP, ALL),
            held(ALL, CAP),
            held(CAP, ALL),
            held32(CAP, 1),
            held32(CAP, 1),
            held32(CAP, CAP),
            held32(TOK, WIDTH),
            held32(2, PIECES, TOK, SIDE),
            held(2, PIECES, 2, TOK, SIDE),
            held(2, PIECES, 2, TOK, SIDE),
            held(2, PIECES, TOK, SIDE),
            held(2, PIECES, TOK, SIDE),
            held(TOK, PIECE),
            held(HALF, 2 * HIDDEN),
            held(HALF, 2 * HIDDEN),
            held(HIDDEN, HALF),
            held(HIDDEN, HALF),
            held32(8, TOK),
            held32(3, 8, TOK),
            held32(8, TOK),
            held32(16 * 8, TOK),
            held(TOK, WIDTH),
            held(TOK, WIDTH),
            dma((3,)),
            dma((4,)),
            dma((4,)),
            dma((PIECES,)),
            dma((PIECES,)),
            dma((3,)),
            dma((3,)),
            dma((3,)),
            dma((4, 4)),
            dma((4, 4)),
            dma((2, PIECES, 2)),
            dma((2, PIECES, 2)),
            dma((2, PIECES)),
            dma((2, PIECES)),
            dma((2,)),
            dma((2,)),
            dma((2,)),
            dma((3,)),
            dma((3,)),
            dma,
            dma,
            dma((PIECES,)),
            dma((PIECES,)),
        ],
        compiler_params=pltpu.CompilerParams(
            collective_id=0, has_side_effects=True, vmem_limit_bytes=56 * 2**20
        ),
        cost_estimate=pl.CostEstimate(
            flops=8_000_000_000, bytes_accessed=8_000_000, transcendentals=131072
        ),
    )(
        layer_input[0, 0],
        grad_output[0, 0],
        selections[0, 0],
        gate_values[0, 0],
        gate_weight[0, 0],
        up_weight[0, 0],
        down_weight[0, 0],
    )

    def blocks(*dims):
        return pl.BlockSpec(dims, lambda i: (i, 0))

    fixed = pl.BlockSpec((16, CAP), lambda i: (0, 0))

    outs = pl.pallas_call(
        finish,
        grid=(2,),
        out_shape=(
            shape((TOK, WIDTH), BF16),
            shape((16, CAP), F32),
            shape((HALF, HIDDEN), F32),
            shape((HALF, HIDDEN), F32),
            shape((HIDDEN, HALF), F32),
        ),
        in_specs=[
            blocks(TOK // 2, WIDTH),
            fixed,
            blocks(HALF // 2, 2 * HIDDEN),
            blocks(HALF // 2, 2 * HIDDEN),
            blocks(HIDDEN // 2, HALF),
            blocks(HIDDEN // 2, HALF),
        ],
        out_specs=(
            blocks(TOK // 2, WIDTH),
            fixed,
            blocks(HALF // 2, HIDDEN),
            blocks(HALF // 2, HIDDEN),
            blocks(HIDDEN // 2, HALF),
        ),
        compiler_params=pltpu.CompilerParams(vmem_limit_bytes=60 * 2**20),
        cost_estimate=pl.CostEstimate(
            flops=1_000_000, bytes_accessed=7_500_000, transcendentals=0
        ),
    )(*middle)
    return tuple(out[None, None] for out in outs)


def solution(mesh):
    return jax.shard_map(
        on_device,
        mesh=mesh,
        in_specs=(
            P("section", "dp", "expert", None),
            P("section", "dp", "expert", None),
            P("section", "dp", None, None),
            P("section", "dp", None, None),
            P("section", "expert", "dp", None),
            P("section", "expert", "dp", None),
            P("section", "expert", None, "dp"),
        ),
        out_specs=(
            P("section", "dp", "expert", None),
            P("section", "dp", None, None),
            P("section", "expert", "dp", None),
            P("section", "expert", "dp", None),
            P("section", "expert", None, "dp"),
        ),
        check_vma=False,
    )
```
